512 devices in a mesh: dom: 16 (over y, x_lo, core), feat: 32 (over x_hi, z).
Axes of the slice: x: 4 (x_hi: 2, x_lo: 2; x = x_hi * 2 + x_lo), y: 4, z: 16, core: 2. Of those that a mesh axis runs over, the one named last changes fastest.
Arguments:
- x0: bfloat16 [6144, 32768], P('dom', 'feat'), may hold values from -6 to 6
- cotangent: bfloat16 [6144, 32768], P('dom', 'feat'), may hold values from -6 to 6
- domain_ids: int32 [6144], P('dom'), may hold values from 0 to 8, as said below
- expert_u: bfloat16 [32768, 4096], P('feat', 'dom'), may hold values from -0.25 to 0.25
- expert_v: bfloat16 [32768, 4096], P('feat', 'dom'), may hold values from -0.03125 to 0.03125
- shared_u: bfloat16 [32768, 512], P(('feat', 'dom')), may hold values from -0.25 to 0.25
- shared_v: bfloat16 [32768, 512], P(('feat', 'dom')), may hold values from -0.03125 to 0.03125
- bias: float32 [2, 32768], P(None, 'feat'), may hold values from -4 to 4
Outputs:
- grad_x0: bfloat16 [6144, 32768], P('dom', 'feat')
- grad_expert_u: bfloat16 [32768, 4096], P('feat', 'dom')
- grad_expert_v: bfloat16 [32768, 4096], P('feat', 'dom')
- grad_shared_u: bfloat16 [32768, 512], P(('feat', 'dom'))
- grad_shared_v: bfloat16 [32768, 512], P(('feat', 'dom'))
- grad_bias: float32 [2, 32768], P(None, 'feat')
The draws below stay inside these ranges and needn't reach their ends.
Inputs may be any that keep to these rules, and one draw needn't show every extreme that they name: `domain_ids`: block k of 384 slots holds first the live examples of domain k // 2, then padding slots marked 8; every block has at least 128 live examples, and block 0 has no padding.
All inputs are finite; a program needn't handle non-finite values.
Results may differ from the reference program's by a relative error of at most 0.009.
Values may be sent and summed in bfloat16 or wider, within the bound.
No kernel may reach another device: no remote copies, remote signals or barrier semaphores. Data moves between devices by JAX's collectives and lax.ppermute only.
A program may use at most 64 MiB of HBM per device.

```python
import jax
import jax.numpy as jnp
from jax import lax

RANK = 512
ROWS = 384
WIDTH = 32768
BATCH = 6144
DOMAINS = 8


def draw_domain_ids(key, part):
    key = jax.random.fold_in(key, 11)
    blocks = BATCH // ROWS
    counts = jax.random.randint(key, (blocks,), ROWS // 3, ROWS + 1)
    counts = counts.at[0].set(ROWS)
    slots = jnp.arange(ROWS, dtype=jnp.int32)[None, :]
    owners = (jnp.arange(blocks, dtype=jnp.int32) // 2)[:, None]
    filled = jnp.where(slots < counts[:, None], owners, DOMAINS)
    return filled.reshape(-1).astype(jnp.int32)


def raised(entries, stream_key, source, target, shards_of, factor):
    owner, partner = [(jnp.arange(entries.shape[dim]) // (entries.shape[dim] // shards_of)).reshape([-1 if axis == dim else 1 for axis in range(entries.ndim)]) for dim in (source, target)]
    chosen = jax.random.permutation(stream_key, shards_of)[partner]
    strong = (owner == chosen) | (owner == (partner + shards_of // 2) % shards_of)
    return jnp.where(strong, factor * entries, entries)


def level_of(key, shape, pieces, least, top_value):
    def one(position, blocks):
        draws = jax.random.uniform(jax.random.fold_in(jax.random.fold_in(key, 6), position), (blocks,), jnp.float32, least / len(pieces), top_value / len(pieces))
        return jnp.repeat(jnp.exp(draws), shape[position] // blocks).reshape((-1,) + (1,) * (len(shape) - position - 1))

    level = one(*pieces[0])
    for cut in pieces[1:]:
        level = level * one(*cut)
    return level


def bell_draw(own_key, dims, deviation, most, shards=(), kind=jnp.bfloat16):
    loudness = level_of(own_key, dims, shards, -0.22, 0.18) if shards else 1.0
    array = jax.random.normal(own_key, dims, jnp.float32) * deviation * loudness
    return jnp.minimum(jnp.maximum(array, -most), most).astype(kind)


def gaussian_with(own_key, extent, scale, reach, cuts, heavy, kind=jnp.bfloat16):
    drawn = scale * jax.random.normal(own_key, extent, jnp.float32)
    if cuts:
        drawn = drawn * level_of(own_key, extent, cuts, -0.22, 0.18)
    return jnp.clip(raised(drawn, jax.random.fold_in(own_key, 3), *heavy), -reach, reach).astype(kind)


def setup_inputs(seed: int = 0) -> dict:
    key_of = jax.random.split(jax.random.key(seed), 9)
    return {
        "x0": bell_draw(key_of[0], (BATCH, WIDTH), 1.0, 6.0, ((0, 16), (1, 32))),
        "cotangent": gaussian_with(key_of[1], (BATCH, WIDTH), 1.0, 6.0, ((0, 16), (1, 32)), (0, 1, 32, 2.75)),
        "domain_ids": draw_domain_ids(jax.random.fold_in(key_of[8], 71), 0),
        "expert_u": bell_draw(key_of[3], (WIDTH, DOMAINS * RANK), RANK ** -0.5, 0.25, ((0, 32), (1, 16))),
        "expert_v": bell_draw(key_of[4], (WIDTH, DOMAINS * RANK), WIDTH ** -0.5, 0.03125, ((0, 32), (1, 16))),
        "shared_u": bell_draw(key_of[5], (WIDTH, RANK), RANK ** -0.5, 0.25, ((0, 512),)),
        "shared_v": bell_draw(key_of[6], (WIDTH, RANK), WIDTH ** -0.5, 0.03125, ((0, 512),)),
        "bias": bell_draw(key_of[7], (2, WIDTH), 1.0, 4.0, ((1, 32),), jnp.float32),
    }


def transposed_dot(left_side, right_side):
    return lax.dot_general(left_side, right_side, (((0,), (0,)), ((), ())), preferred_element_type=jnp.float32)


def cross_dot(left_side, right_side):
    return lax.dot_general(left_side, right_side, (((1,), (1,)), ((), ())), preferred_element_type=jnp.float32)


def reference(x0, cotangent, domain_ids, expert_u, expert_v, shared_u, shared_v, bias):
    blocks = BATCH // ROWS
    x_blocks = x0.reshape(blocks, ROWS, WIDTH)
    cot_blocks = cotangent.reshape(blocks, ROWS, WIDTH)
    id_blocks = domain_ids.reshape(blocks, ROWS)

    def block_step(totals, block_item):
        block_index, inputs_low, cot_low, ids_block = block_item
        domain = (block_index // 2).astype(jnp.int32)
        start_col = (domain * RANK).astype(jnp.int32)
        dom_u = lax.dynamic_slice_in_dim(expert_u, start_col, RANK, 1)
        dom_v = lax.dynamic_slice_in_dim(expert_v, start_col, RANK, 1)
        live_rows = (ids_block == domain)[:, None]
        masked = jnp.where(live_rows, cot_low, jnp.zeros_like(cot_low))
        inputs = inputs_low.astype(jnp.float32)
        first_rank = jnp.dot(inputs_low, dom_v, preferred_element_type=jnp.float32).astype(jnp.bfloat16)
        first_gate = cross_dot(first_rank, dom_u) + bias[0][None, :]
        layer_one = (inputs * first_gate + inputs).astype(jnp.bfloat16)
        second_rank = jnp.dot(layer_one, shared_v, preferred_element_type=jnp.float32).astype(jnp.bfloat16)
        second_gate = cross_dot(second_rank, shared_u) + bias[1][None, :]
        masked_wide = masked.astype(jnp.float32)
        second_adj = (masked_wide * inputs).astype(jnp.bfloat16)
        back_two = jnp.dot(second_adj, shared_u, preferred_element_type=jnp.float32).astype(jnp.bfloat16)
        layer_grad = masked_wide + cross_dot(back_two, shared_v)
        first_adj = (layer_grad * inputs).astype(jnp.bfloat16)
        back_one = jnp.dot(first_adj, dom_u, preferred_element_type=jnp.float32).astype(jnp.bfloat16)
        grad_inputs = masked_wide * second_gate + layer_grad * first_gate + layer_grad + cross_dot(back_one, dom_v)
        term_su = transposed_dot(second_adj, second_rank)
        term_sv = transposed_dot(layer_one, back_two)
        part_u = transposed_dot(first_adj, first_rank)
        part_v = transposed_dot(inputs_low, back_one)
        bias_terms = jnp.stack([jnp.sum(first_adj.astype(jnp.float32), axis=0), jnp.sum(second_adj.astype(jnp.float32), axis=0)])
        new_totals = (totals[0] + term_su, totals[1] + term_sv, totals[2] + bias_terms)
        return new_totals, (grad_inputs.astype(jnp.bfloat16), part_u, part_v)

    start_totals = (jnp.zeros((WIDTH, RANK), jnp.float32), jnp.zeros((WIDTH, RANK), jnp.float32), jnp.zeros((2, WIDTH), jnp.float32))
    block_ids = jnp.arange(blocks, dtype=jnp.int32)
    totals, outputs = lax.scan(block_step, start_totals, (block_ids, x_blocks, cot_blocks, id_blocks))
    grad_inputs, parts_u, parts_v = outputs

    def pair_up(parts):
        paired = parts.reshape(DOMAINS, 2, WIDTH, RANK)
        summed = (paired[:, 0] + paired[:, 1]).astype(jnp.bfloat16)
        return jnp.transpose(summed, (1, 0, 2)).reshape(WIDTH, DOMAINS * RANK)

    return (grad_inputs.reshape(BATCH, WIDTH), pair_up(parts_u), pair_up(parts_v),
            totals[0].astype(jnp.bfloat16), totals[1].astype(jnp.bfloat16), totals[2])
```

```python
import jax
import jax.numpy as jnp
from jax import lax
from jax.sharding import PartitionSpec as P

FAR = 2


def partner_swap(value):
    pairs = [(source, source ^ 1) for source in range(lax.axis_size("dom"))]
    return lax.ppermute(value, "dom", pairs)


def near_groups():
    half = lax.axis_size("feat") // FAR
    return [[far * half + 2 * pair + bit for far in range(FAR) for bit in range(2)] for pair in range(half // 2)]


def ring_groups():
    half = lax.axis_size("feat") // FAR
    return [[far * half + 2 * step + bit for step in range(half // 2)] for far in range(FAR) for bit in range(2)]


def exchange(value, axis, groups=None):
    return lax.all_to_all(value, axis, 0, 0, axis_index_groups=groups, tiled=True)


def summed(value, axis, groups, members):
    rows = value.shape[0] // members
    pieces = exchange(value, axis, groups).reshape(members, rows, value.shape[1])
    return jnp.sum(pieces.astype(jnp.float32), axis=0).astype(jnp.bfloat16)


def gathered(value, axis, groups, members):
    repeated = jnp.broadcast_to(value[None], (members, *value.shape))
    return exchange(repeated.reshape(members * value.shape[0], value.shape[1]), axis, groups)


def feature_sum(value):
    near, ring = near_groups(), ring_groups()
    part = summed(value, "feat", near, len(near[0]))
    part = summed(part, "feat", ring, len(ring[0]))
    part = gathered(part, "feat", ring, len(ring[0]))
    return gathered(part, "feat", near, len(near[0]))


def dot(left_side, right_side):
    return jnp.dot(left_side, right_side, preferred_element_type=jnp.float32)


def transposed_dot(left_side, right_side):
    return lax.dot_general(
        left_side, right_side, (((0,), (0,)), ((), ())), preferred_element_type=jnp.float32
    )


def cross_dot(left_side, right_side):
    return lax.dot_general(
        left_side, right_side, (((1,), (1,)), ((), ())), preferred_element_type=jnp.float32
    )


def local(x0, cotangent, domain_ids, expert_u, expert_v, shared_u, shared_v, bias):
    low = jnp.bfloat16
    rows, width = x0.shape
    half_rank = expert_u.shape[1]
    rank = 2 * half_rank
    members = lax.axis_size("dom")
    domain = lax.axis_index("dom") // 2
    other_v = partner_swap(expert_v)
    other_u = partner_swap(expert_u)
    full_v = jnp.concatenate([expert_v, other_v], 1)
    full_u = jnp.concatenate([expert_u, other_u], 1)
    whole_sv = lax.all_gather(shared_v, "dom", axis=0, tiled=True)
    whole_su = gathered(shared_u, "dom", None, members)
    live_rows = (domain_ids == domain)[:, None]
    masked = jnp.where(live_rows, cotangent, jnp.zeros_like(cotangent))
    masked_wide = masked.astype(jnp.float32)
    inputs = x0.astype(jnp.float32)
    second_adj = (masked_wide * inputs).astype(low)
    first_part = dot(x0, full_v).astype(low)
    back_two_part = dot(second_adj, whole_su).astype(low)
    sums = feature_sum(jnp.concatenate([first_part, back_two_part], 0))
    first_rank, back_two = sums[:rows], sums[rows:]
    first_gate = cross_dot(first_rank, full_u) + bias[0][None, :]
    layer_one = (inputs * first_gate + inputs).astype(low)
    layer_grad = masked_wide + cross_dot(back_two, whole_sv)
    first_adj = (layer_grad * inputs).astype(low)
    second_part = dot(layer_one, whole_sv).astype(low)
    back_one_part = dot(first_adj, full_u).astype(low)
    partial_gu = transposed_dot(first_adj, first_rank)
    peer_gu = partner_swap(partial_gu[:, half_rank:].astype(low))
    grad_eu = (partial_gu[:, :half_rank] + peer_gu.astype(jnp.float32)).astype(low)
    term_sv = transposed_dot(layer_one, back_two)
    sum_sv = lax.psum_scatter(term_sv, "dom", scatter_dimension=0, tiled=True)
    sums = feature_sum(jnp.concatenate([second_part, back_one_part], 0))
    second_rank, back_one = sums[:rows], sums[rows:]
    partial_gv = transposed_dot(x0, back_one)
    peer_gv = partner_swap(partial_gv[:, half_rank:].astype(low))
    grad_ev = (partial_gv[:, :half_rank] + peer_gv.astype(jnp.float32)).astype(low)
    second_gate = cross_dot(second_rank, whole_su) + bias[1][None, :]
    grad_inputs = (
        masked_wide * second_gate
        + layer_grad * first_gate
        + layer_grad
        + cross_dot(back_one, full_v)
    ).astype(low)
    bias_terms = jnp.stack(
        [
            jnp.sum(first_adj.astype(jnp.float32), axis=0),
            jnp.sum(second_adj.astype(jnp.float32), axis=0),
        ]
    )
    bias_high = bias_terms.astype(low)
    bias_rest = (bias_terms - bias_high.astype(jnp.float32)).astype(low)
    bias_lines = jnp.stack([bias_high, bias_rest]).reshape(4 * width // rank, rank)
    term_su = transposed_dot(second_adj, second_rank).astype(low).reshape(members, width // members, rank)
    lines = bias_lines.shape[0]
    sent = jnp.concatenate([term_su, jnp.broadcast_to(bias_lines[None], (members, lines, rank))], 1)
    taken = exchange(sent, "dom").astype(jnp.float32).sum(0)
    sum_su = taken[: width // members]
    bias_sum = taken[width // members :].reshape(2, 2, width)
    grad_bias = bias_sum[0] + bias_sum[1]
    return (
        grad_inputs,
        grad_eu,
        grad_ev,
        sum_su.astype(low),
        sum_sv.astype(low),
        grad_bias,
    )


def solution(mesh):
    placed = (
        P("dom", "feat"),
        P("dom", "feat"),
        P("dom"),
        P("feat", "dom"),
        P("feat", "dom"),
        P(("feat", "dom"), None),
        P(("feat", "dom"), None),
        P(None, "feat"),
    )
    return jax.shard_map(
        local,
        mesh=mesh,
        in_specs=placed,
        out_specs=(
            P("dom", "feat"),
            P("feat", "dom"),
            P("feat", "dom"),
            P(("feat", "dom"), None),
            P(("feat", "dom"), None),
            P(None, "feat"),
        ),
        check_vma=False,
    )
```

```python
import jax
import jax.numpy as jnp
from jax import lax
from jax.sharding import PartitionSpec as P

FAR = 2


def partner_swap(value):
    pairs = [(source, source ^ 1) for source in range(lax.axis_size("dom"))]
    return lax.ppermute(value, "dom", pairs)


def near_groups():
    half = lax.axis_size("feat") // FAR
    return [[far * half + 2 * pair + bit for far in range(FAR) for bit in range(2)] for pair in range(half // 2)]


def ring_groups():
    half = lax.axis_size("feat") // FAR
    return [[far * half + 2 * step + bit for step in range(half // 2)] for far in range(FAR) for bit in range(2)]


def chip_groups():
    return [list(range(core, lax.axis_size("dom"), 2)) for core in range(2)]


def exchange(value, axis, groups=None):
    return lax.all_to_all(value, axis, 0, 0, axis_index_groups=groups, tiled=True)


def summed(value, axis, groups, members):
    rows = value.shape[0] // members
    pieces = exchange(value, axis, groups).reshape(members, rows, value.shape[1])
    return jnp.sum(pieces.astype(jnp.float32), axis=0).astype(jnp.bfloat16)


def gathered(value, axis, groups, members):
    repeated = jnp.broadcast_to(value[None], (members, *value.shape))
    return exchange(repeated.reshape(members * value.shape[0], value.shape[1]), axis, groups)


def feature_sum(value):
    near, ring = near_groups(), ring_groups()
    part = summed(value, "feat", near, len(near[0]))
    part = summed(part, "feat", ring, len(ring[0]))
    part = gathered(part, "feat", ring, len(ring[0]))
    return gathered(part, "feat", near, len(near[0]))


def dot(left_side, right_side):
    return jnp.dot(left_side, right_side, preferred_element_type=jnp.float32)


def transposed_dot(left_side, right_side):
    return lax.dot_general(
        left_side, right_side, (((0,), (0,)), ((), ())), preferred_element_type=jnp.float32
    )


def cross_dot(left_side, right_side):
    return lax.dot_general(
        left_side, right_side, (((1,), (1,)), ((), ())), preferred_element_type=jnp.float32
    )


def local(x0, cotangent, domain_ids, expert_u, expert_v, shared_u, shared_v, bias):
    low = jnp.bfloat16
    rows, width = x0.shape
    half_rank = expert_u.shape[1]
    rank = 2 * half_rank
    members = lax.axis_size("dom")
    domain = lax.axis_index("dom") // 2
    other_v = partner_swap(expert_v)
    other_u = partner_swap(expert_u)
    full_v = jnp.concatenate([expert_v, other_v], 1)
    full_u = jnp.concatenate([expert_u, other_u], 1)
    lines = shared_u.shape[0]
    own_maps = gathered(jnp.concatenate([shared_u, shared_v], 0), "dom", chip_groups(), members // 2)
    own_maps = own_maps.reshape(members // 2, 2, lines, rank)
    is_first = lax.axis_index("dom") % 2 == 0

    def whole(own):
        other = partner_swap(own)
        pair = [jnp.where(is_first, own, other), jnp.where(is_first, other, own)]
        return jnp.stack(pair, 1).reshape(width, rank)

    whole_su, whole_sv = whole(own_maps[:, 0]), whole(own_maps[:, 1])
    live_rows = (domain_ids == domain)[:, None]
    masked = jnp.where(live_rows, cotangent, jnp.zeros_like(cotangent))
    masked_wide = masked.astype(jnp.float32)
    inputs = x0.astype(jnp.float32)
    second_adj = (masked_wide * inputs).astype(low)
    first_part = dot(x0, full_v).astype(low)
    back_two_part = dot(second_adj, whole_su).astype(low)
    sums = feature_sum(jnp.concatenate([first_part, back_two_part], 0))
    first_rank, back_two = sums[:rows], sums[rows:]
    first_gate = cross_dot(first_rank, full_u) + bias[0][None, :]
    layer_one = (inputs * first_gate + inputs).astype(low)
    layer_grad = masked_wide + cross_dot(back_two, whole_sv)
    first_adj = (layer_grad * inputs).astype(low)
    second_part = dot(layer_one, whole_sv).astype(low)
    back_one_part = dot(first_adj, full_u).astype(low)
    partial_gu = transposed_dot(first_adj, first_rank)
    peer_gu = partner_swap(partial_gu[:, half_rank:].astype(low))
    grad_eu = (partial_gu[:, :half_rank] + peer_gu.astype(jnp.float32)).astype(low)
    term_sv = transposed_dot(layer_one, back_two)
    sum_sv = lax.psum_scatter(term_sv, "dom", scatter_dimension=0, tiled=True)
    sums = feature_sum(jnp.concatenate([second_part, back_one_part], 0))
    second_rank, back_one = sums[:rows], sums[rows:]
    partial_gv = transposed_dot(x0, back_one)
    peer_gv = partner_swap(partial_gv[:, half_rank:].astype(low))
    grad_ev = (partial_gv[:, :half_rank] + peer_gv.astype(jnp.float32)).astype(low)
    second_gate = cross_dot(second_rank, whole_su) + bias[1][None, :]
    grad_inputs = (
        masked_wide * second_gate
        + layer_grad * first_gate
        + layer_grad
        + cross_dot(back_one, full_v)
    ).astype(low)
    bias_terms = jnp.stack(
        [
            jnp.sum(first_adj.astype(jnp.float32), axis=0),
            jnp.sum(second_adj.astype(jnp.float32), axis=0),
        ]
    )
    bias_high = bias_terms.astype(low)
    bias_rest = (bias_terms - bias_high.astype(jnp.float32)).astype(low)
    bias_lines = jnp.stack([bias_high, bias_rest]).reshape(4 * width // rank, rank)
    term_su = transposed_dot(second_adj, second_rank).astype(low).reshape(members, width // members, rank)
    lines = bias_lines.shape[0]
    sent = jnp.concatenate([term_su, jnp.broadcast_to(bias_lines[None], (members, lines, rank))], 1)
    taken = exchange(sent, "dom").astype(jnp.float32).sum(0)
    sum_su = taken[: width // members]
    bias_sum = taken[width // members :].reshape(2, 2, width)
    grad_bias = bias_sum[0] + bias_sum[1]
    return (
        grad_inputs,
        grad_eu,
        grad_ev,
        sum_su.astype(low),
        sum_sv.astype(low),
        grad_bias,
    )


def solution(mesh):
    placed = (
        P("dom", "feat"),
        P("dom", "feat"),
        P("dom"),
        P("feat", "dom"),
        P("feat", "dom"),
        P(("feat", "dom"), None),
        P(("feat", "dom"), None),
        P(None, "feat"),
    )
    return jax.shard_map(
        local,
        mesh=mesh,
        in_specs=placed,
        out_specs=(
            P("dom", "feat"),
            P("feat", "dom"),
            P("feat", "dom"),
            P(("feat", "dom"), None),
            P(("feat", "dom"), None),
            P(None, "feat"),
        ),
        check_vma=False,
    )
```

```python
import jax
import jax.numpy as jnp
from jax import lax
from jax.sharding import PartitionSpec as P

FAR = 2


def core_swap(value):
    pairs = [(source, source ^ 1) for source in range(lax.axis_size("dom"))]
    return lax.ppermute(value, "dom", pairs)


def far_swap(value):
    count = lax.axis_size("feat")
    return lax.ppermute(value, "feat", [(source, (source + count // FAR) % count) for source in range(count)])


def line_groups():
    length = lax.axis_size("feat") // FAR
    return [list(range(far * length, (far + 1) * length)) for far in range(FAR)]


def chip_groups():
    return [list(range(core, lax.axis_size("dom"), 2)) for core in range(2)]


def exchange(value, axis, groups):
    return lax.all_to_all(value, axis, 0, 0, axis_index_groups=groups, tiled=True)


def gathered(value, axis, groups):
    members = len(groups[0])
    repeated = jnp.broadcast_to(value[None], (members, *value.shape))
    return exchange(repeated.reshape(members * value.shape[0], value.shape[1]), axis, groups)


def line_sum(value):
    groups = line_groups()
    members = len(groups[0])
    pieces = exchange(value, "feat", groups).reshape(members, -1, value.shape[1])
    part = jnp.sum(pieces.astype(jnp.float32), axis=0).astype(jnp.bfloat16)
    return gathered(part, "feat", groups)


def dot(left_side, right_side):
    return jnp.dot(left_side, right_side, preferred_element_type=jnp.float32)


def transposed_dot(left_side, right_side):
    return lax.dot_general(
        left_side, right_side, (((0,), (0,)), ((), ())), preferred_element_type=jnp.float32
    )


def cross_dot(left_side, right_side):
    return lax.dot_general(
        left_side, right_side, (((1,), (1,)), ((), ())), preferred_element_type=jnp.float32
    )


def local(x0, cotangent, domain_ids, expert_u, expert_v, shared_u, shared_v, bias):
    low = jnp.bfloat16
    wide = jnp.float32
    rows, width = x0.shape
    half_rows = rows // 2
    half_rank = expert_u.shape[1]
    rank = 2 * half_rank
    chips = lax.axis_size("dom") // 2
    lines = shared_u.shape[0]
    domain = lax.axis_index("dom") // 2
    core = lax.axis_index("dom") % 2
    far = lax.axis_index("feat") // (lax.axis_size("feat") // FAR)

    def halves(value):
        return [
            lax.dynamic_slice_in_dim(value, place * half_rows, half_rows, 0) for place in (far, 1 - far)
        ]

    own_maps = gathered(jnp.concatenate([shared_u, shared_v], 0), "dom", chip_groups())
    own_maps = own_maps.reshape(chips, 2, lines, rank)
    other_v = core_swap(expert_v)
    other_u = core_swap(expert_u)
    full_v = jnp.concatenate([expert_v, other_v], 1)
    full_u = jnp.concatenate([expert_u, other_u], 1)

    def whole(own, other):
        pair = [jnp.where(core == 0, own, other), jnp.where(core == 0, other, own)]
        return jnp.stack(pair, 1).reshape(width, rank)

    x_halves = halves(x0)
    inputs = [x.astype(wide) for x in x_halves]
    live = [(ids == domain)[:, None] for ids in halves(domain_ids)]
    masked = [jnp.where(on, cot, jnp.zeros_like(cot)).astype(wide) for on, cot in zip(live, halves(cotangent))]
    second_adj = [(m * x).astype(low) for m, x in zip(masked, inputs)]

    first_away = far_swap(dot(x_halves[1], full_v).astype(low))
    first_half = dot(x_halves[0], full_v) + first_away.astype(wide)
    whole_su = whole(own_maps[:, 0], core_swap(own_maps[:, 0]))
    back_away = far_swap(dot(second_adj[1], whole_su).astype(low))
    back_half = dot(second_adj[0], whole_su) + back_away.astype(wide)
    own_sums = jnp.concatenate([first_half.astype(low), back_half.astype(low)], 0)
    own_sv, own_sums = lax.optimization_barrier((own_maps[:, 1], own_sums))
    whole_sv = whole(own_sv, core_swap(own_sv))
    own_sums = line_sum(own_sums)
    sums = [own_sums, far_swap(own_sums)]
    first_rank = [s[:half_rows] for s in sums]
    back_two = [s[half_rows:] for s in sums]

    def middle(i):
        first_gate = cross_dot(first_rank[i], full_u) + bias[0][None, :]
        layer_one = (inputs[i] * first_gate + inputs[i]).astype(low)
        layer_grad = masked[i] + cross_dot(back_two[i], whole_sv)
        first_adj = (layer_grad * inputs[i]).astype(low)
        parts = [dot(layer_one, whole_sv), dot(first_adj, full_u)]
        return first_gate, layer_one, layer_grad, first_adj, parts

    first_gate, layer_one, layer_grad, first_adj, parts = zip(middle(0), middle(1))
    away = far_swap(jnp.concatenate([p.astype(low) for p in parts[1]], 0)).astype(wide)
    own_sums = jnp.concatenate(
        [
            (parts[0][0] + away[:half_rows]).astype(low),
            (parts[0][1] + away[half_rows:]).astype(low),
        ],
        0,
    )
    own_sums = line_sum(own_sums)

    def row_sum(left_side, right_side):
        return sum(transposed_dot(a, b) for a, b in zip(left_side, right_side))

    def with_partner(partial):
        peer = core_swap(partial[:, half_rank:].astype(low))
        return (partial[:, :half_rank] + peer.astype(wide)).astype(low)

    def chip_part(term):
        blocks = term.reshape(chips, 2, lines, rank)
        keep, give = [
            lax.dynamic_index_in_dim(blocks, place, 1, keepdims=False) for place in (core, 1 - core)
        ]
        return (keep + core_swap(give.astype(low)).astype(wide)).astype(low)

    grad_eu = with_partner(row_sum(first_adj, first_rank))
    part_sv = chip_part(row_sum(layer_one, back_two))
    bias_terms = jnp.stack(
        [sum(jnp.sum(a.astype(wide), axis=0) for a in adj) for adj in (first_adj, second_adj)]
    )
    bias_terms = bias_terms + core_swap(bias_terms)
    bias_high = bias_terms.astype(low)
    bias_rest = (bias_terms - bias_high.astype(wide)).astype(low)
    bias_lines = jnp.stack([bias_high, bias_rest]).reshape(4 * width // rank, rank)
    bias_lines = jnp.broadcast_to(bias_lines[None], (chips, *bias_lines.shape))

    sums = [own_sums, far_swap(own_sums)]
    second_rank = [s[:half_rows] for s in sums]
    back_one = [s[half_rows:] for s in sums]
    part_su = chip_part(row_sum(second_adj, second_rank))
    sent = jnp.concatenate([part_su, part_sv, bias_lines], 1)
    taken = exchange(sent.reshape(-1, rank), "dom", chip_groups()).reshape(sent.shape)
    taken = jnp.sum(taken.astype(wide), axis=0)
    bias_sum = taken[2 * lines :].reshape(2, 2, width)
    grad_ev = with_partner(row_sum(x_halves, back_one))
    grad_inputs = jnp.zeros((rows, width), low)
    for i, place in enumerate((far, 1 - far)):
        second_gate = cross_dot(second_rank[i], whole_su) + bias[1][None, :]
        grad_half = (
            masked[i] * second_gate
            + layer_grad[i] * first_gate[i]
            + layer_grad[i]
            + cross_dot(back_one[i], full_v)
        ).astype(low)
        grad_inputs = lax.dynamic_update_slice_in_dim(grad_inputs, grad_half, place * half_rows, 0)
    return (
        grad_inputs,
        grad_eu,
        grad_ev,
        taken[:lines].astype(low),
        taken[lines : 2 * lines].astype(low),
        bias_sum[0] + bias_sum[1],
    )


def solution(mesh):
    placed = (
        P("dom", "feat"),
        P("dom", "feat"),
        P("dom"),
        P("feat", "dom"),
        P("feat", "dom"),
        P(("feat", "dom"), None),
        P(("feat", "dom"), None),
        P(None, "feat"),
    )
    return jax.shard_map(
        local,
        mesh=mesh,
        in_specs=placed,
        out_specs=(
            P("dom", "feat"),
            P("feat", "dom"),
            P("feat", "dom"),
            P(("feat", "dom"), None),
            P(("feat", "dom"), None),
            P(None, "feat"),
        ),
        check_vma=False,
    )
```

```python
import jax
import jax.numpy as jnp
from jax import lax
from jax.sharding import PartitionSpec as P

FAR = 2


def core_swap(value):
    pairs = [(source, source ^ 1) for source in range(lax.axis_size("dom"))]
    return lax.ppermute(value, "dom", pairs)


def near_groups():
    half = lax.axis_size("feat") // FAR
    return [[far * half + 2 * pair + bit for far in range(FAR) for bit in range(2)] for pair in range(half // 2)]


def ring_groups():
    half = lax.axis_size("feat") // FAR
    return [[far * half + 2 * step + bit for step in range(half // 2)] for far in range(FAR) for bit in range(2)]


def chip_groups():
    return [list(range(core, lax.axis_size("dom"), 2)) for core in range(2)]


def exchange(value, axis, groups):
    return lax.all_to_all(value, axis, 0, 0, axis_index_groups=groups, tiled=True)


def gathered(value, axis, groups):
    members = len(groups[0])
    repeated = jnp.broadcast_to(value[None], (members, *value.shape))
    return exchange(repeated.reshape(members * value.shape[0], value.shape[1]), axis, groups)


def summed(value, axis, groups):
    pieces = exchange(value, axis, groups).reshape(len(groups[0]), -1, value.shape[1])
    return jnp.sum(pieces.astype(jnp.float32), axis=0).astype(jnp.bfloat16)


def feature_sum(value):
    near, ring = near_groups(), ring_groups()
    part = summed(summed(value, "feat", near), "feat", ring)
    return gathered(gathered(part, "feat", ring), "feat", near)


def dot(left_side, right_side):
    return jnp.dot(left_side, right_side, preferred_element_type=jnp.float32)


def transposed_dot(left_side, right_side):
    return lax.dot_general(
        left_side, right_side, (((0,), (0,)), ((), ())), preferred_element_type=jnp.float32
    )


def cross_dot(left_side, right_side):
    return lax.dot_general(
        left_side, right_side, (((1,), (1,)), ((), ())), preferred_element_type=jnp.float32
    )


def local(x0, cotangent, domain_ids, expert_u, expert_v, shared_u, shared_v, bias):
    low = jnp.bfloat16
    wide = jnp.float32
    rows, width = x0.shape
    half_rank = expert_u.shape[1]
    rank = 2 * half_rank
    chips = lax.axis_size("dom") // 2
    lines = shared_u.shape[0]
    domain = lax.axis_index("dom") // 2
    core = lax.axis_index("dom") % 2

    own_maps = gathered(jnp.concatenate([shared_u, shared_v], 0), "dom", chip_groups())
    own_maps = own_maps.reshape(chips, 2, lines, rank)
    other_v = core_swap(expert_v)
    other_u = core_swap(expert_u)
    full_v = jnp.concatenate([expert_v, other_v], 1)
    full_u = jnp.concatenate([expert_u, other_u], 1)

    def whole(own, other):
        pair = [jnp.where(core == 0, own, other), jnp.where(core == 0, other, own)]
        return jnp.stack(pair, 1).reshape(width, rank)

    masked = jnp.where((domain_ids == domain)[:, None], cotangent, jnp.zeros_like(cotangent)).astype(wide)
    inputs = x0.astype(wide)
    second_adj = (masked * inputs).astype(low)

    first_part = dot(x0, full_v).astype(low)
    whole_su = whole(own_maps[:, 0], core_swap(own_maps[:, 0]))
    back_two_part = dot(second_adj, whole_su).astype(low)
    both = jnp.concatenate([first_part, back_two_part], 0)
    own_sv, both = lax.optimization_barrier((own_maps[:, 1], both))
    whole_sv = whole(own_sv, core_swap(own_sv))
    sums = feature_sum(both)
    first_rank, back_two = sums[:rows], sums[rows:]
    first_gate = cross_dot(first_rank, full_u) + bias[0][None, :]
    layer_one = (inputs * first_gate + inputs).astype(low)
    layer_grad = masked + cross_dot(back_two, whole_sv)
    first_adj = (layer_grad * inputs).astype(low)
    second_part = dot(layer_one, whole_sv).astype(low)
    back_one_part = dot(first_adj, full_u).astype(low)
    sums = feature_sum(jnp.concatenate([second_part, back_one_part], 0))

    def with_partner(partial):
        peer = core_swap(partial[:, half_rank:].astype(low))
        return (partial[:, :half_rank] + peer.astype(wide)).astype(low)

    def chip_part(term):
        blocks = term.reshape(chips, 2, lines, rank)
        keep, give = [
            lax.dynamic_index_in_dim(blocks, place, 1, keepdims=False) for place in (core, 1 - core)
        ]
        return (keep + core_swap(give.astype(low)).astype(wide)).astype(low)

    grad_eu = with_partner(transposed_dot(first_adj, first_rank))
    part_sv = chip_part(transposed_dot(layer_one, back_two))
    bias_terms = jnp.stack([jnp.sum(a.astype(wide), axis=0) for a in (first_adj, second_adj)])
    bias_terms = bias_terms + core_swap(bias_terms)
    bias_high = bias_terms.astype(low)
    bias_rest = (bias_terms - bias_high.astype(wide)).astype(low)
    bias_lines = jnp.stack([bias_high, bias_rest]).reshape(4 * width // rank, rank)
    bias_lines = jnp.broadcast_to(bias_lines[None], (chips, *bias_lines.shape))

    second_rank, back_one = sums[:rows], sums[rows:]
    part_su = chip_part(transposed_dot(second_adj, second_rank))
    sent = jnp.concatenate([part_su, part_sv, bias_lines], 1)
    taken = exchange(sent.reshape(-1, rank), "dom", chip_groups()).reshape(sent.shape)
    taken = jnp.sum(taken.astype(wide), axis=0)
    bias_sum = taken[2 * lines :].reshape(2, 2, width)
    grad_ev = with_partner(transposed_dot(x0, back_one))
    second_gate = cross_dot(second_rank, whole_su) + bias[1][None, :]
    grad_inputs = (
        masked * second_gate + layer_grad * first_gate + layer_grad + cross_dot(back_one, full_v)
    ).astype(low)
    return (
        grad_inputs,
        grad_eu,
        grad_ev,
        taken[:lines].astype(low),
        taken[lines : 2 * lines].astype(low),
        bias_sum[0] + bias_sum[1],
    )


def solution(mesh):
    placed = (
        P("dom", "feat"),
        P("dom", "feat"),
        P("dom"),
        P("feat", "dom"),
        P("feat", "dom"),
        P(("feat", "dom"), None),
        P(("feat", "dom"), None),
        P(None, "feat"),
    )
    return jax.shard_map(
        local,
        mesh=mesh,
        in_specs=placed,
        out_specs=(
            P("dom", "feat"),
            P("feat", "dom"),
            P("feat", "dom"),
            P(("feat", "dom"), None),
            P(("feat", "dom"), None),
            P(None, "feat"),
        ),
        check_vma=False,
    )
```

```python
import jax
import jax.numpy as jnp
from jax import lax
from jax.sharding import PartitionSpec as P

FAR = 2


def core_swap(value):
    pairs = [(source, source ^ 1) for source in range(lax.axis_size("dom"))]
    return lax.ppermute(value, "dom", pairs)


def near_groups():
    half = lax.axis_size("feat") // FAR
    return [[far * half + 2 * pair + bit for far in range(FAR) for bit in range(2)] for pair in range(half // 2)]


def ring_groups():
    half = lax.axis_size("feat") // FAR
    return [[far * half + 2 * step + bit for step in range(half // 2)] for far in range(FAR) for bit in range(2)]


def chip_groups():
    return [list(range(core, lax.axis_size("dom"), 2)) for core in range(2)]


def exchange(value, axis, groups):
    return lax.all_to_all(value, axis, 0, 0, axis_index_groups=groups, tiled=True)


def gathered(value, axis, groups):
    members = len(groups[0])
    repeated = jnp.broadcast_to(value[None], (members, *value.shape))
    return exchange(repeated.reshape(members * value.shape[0], value.shape[1]), axis, groups)


def summed(value, axis, groups):
    pieces = exchange(value, axis, groups).reshape(len(groups[0]), -1, value.shape[1])
    return jnp.sum(pieces.astype(jnp.float32), axis=0).astype(jnp.bfloat16)


def feature_sum(value, beside):
    near, ring = near_groups(), ring_groups()
    part = summed(summed(value, "feat", near), "feat", ring)
    part, beside = lax.optimization_barrier((part, beside))
    return gathered(gathered(part, "feat", ring), "feat", near), beside


def dot(left_side, right_side):
    return jnp.dot(left_side, right_side, preferred_element_type=jnp.float32)


def transposed_dot(left_side, right_side):
    return lax.dot_general(
        left_side, right_side, (((0,), (0,)), ((), ())), preferred_element_type=jnp.float32
    )


def cross_dot(left_side, right_side):
    return lax.dot_general(
        left_side, right_side, (((1,), (1,)), ((), ())), preferred_element_type=jnp.float32
    )


def local(x0, cotangent, domain_ids, expert_u, expert_v, shared_u, shared_v, bias):
    low = jnp.bfloat16
    wide = jnp.float32
    rows, width = x0.shape
    half_rank = expert_u.shape[1]
    rank = 2 * half_rank
    chips = lax.axis_size("dom") // 2
    lines = shared_u.shape[0]
    domain = lax.axis_index("dom") // 2
    core = lax.axis_index("dom") % 2

    own_maps = gathered(jnp.concatenate([shared_u, shared_v], 0), "dom", chip_groups())
    own_maps = own_maps.reshape(chips, 2, lines, rank)
    other_v = core_swap(expert_v)
    full_v = jnp.concatenate([expert_v, other_v], 1)

    def whole(own, other):
        pair = [jnp.where(core == 0, own, other), jnp.where(core == 0, other, own)]
        return jnp.stack(pair, 1).reshape(width, rank)

    masked = jnp.where((domain_ids == domain)[:, None], cotangent, jnp.zeros_like(cotangent)).astype(wide)
    inputs = x0.astype(wide)
    second_adj = (masked * inputs).astype(low)

    first_part = dot(x0, full_v).astype(low)
    whole_su = whole(own_maps[:, 0], core_swap(own_maps[:, 0]))
    back_two_part = dot(second_adj, whole_su).astype(low)
    both = jnp.concatenate([first_part, back_two_part], 0)
    own_sv, expert_u, both = lax.optimization_barrier((own_maps[:, 1], expert_u, both))
    whole_sv = whole(own_sv, core_swap(own_sv))
    full_u = jnp.concatenate([expert_u, core_swap(expert_u)], 1)
    sums, (whole_sv, full_u) = feature_sum(both, (whole_sv, full_u))
    first_rank, back_two = sums[:rows], sums[rows:]
    first_gate = cross_dot(first_rank, full_u) + bias[0][None, :]
    layer_one = (inputs * first_gate + inputs).astype(low)
    layer_grad = masked + cross_dot(back_two, whole_sv)
    first_adj = (layer_grad * inputs).astype(low)
    second_part = dot(layer_one, whole_sv).astype(low)
    back_one_part = dot(first_adj, full_u).astype(low)
    both = jnp.concatenate([second_part, back_one_part], 0)

    def with_partner(partial):
        peer = core_swap(partial[:, half_rank:].astype(low))
        return (partial[:, :half_rank] + peer.astype(wide)).astype(low)

    def chip_part(term):
        blocks = term.reshape(chips, 2, lines, rank)
        keep, give = [
            lax.dynamic_index_in_dim(blocks, place, 1, keepdims=False) for place in (core, 1 - core)
        ]
        return (keep + core_swap(give.astype(low)).astype(wide)).astype(low)

    grad_eu = with_partner(transposed_dot(first_adj, first_rank))
    part_sv = chip_part(transposed_dot(layer_one, back_two))
    bias_terms = jnp.stack([jnp.sum(a.astype(wide), axis=0) for a in (first_adj, second_adj)])
    bias_terms = bias_terms + core_swap(bias_terms)
    bias_high = bias_terms.astype(low)
    bias_rest = (bias_terms - bias_high.astype(wide)).astype(low)
    bias_lines = jnp.stack([bias_high, bias_rest]).reshape(4 * width // rank, rank)
    bias_lines = jnp.broadcast_to(bias_lines[None], (chips, *bias_lines.shape))

    sums, (grad_eu, part_sv, bias_lines) = feature_sum(both, (grad_eu, part_sv, bias_lines))
    second_rank, back_one = sums[:rows], sums[rows:]
    part_su = chip_part(transposed_dot(second_adj, second_rank))
    sent = jnp.concatenate([part_su, part_sv, bias_lines], 1)
    sent, second_rank, back_one = lax.optimization_barrier((sent, second_rank, back_one))
    taken = exchange(sent.reshape(-1, rank), "dom", chip_groups()).reshape(sent.shape)
    taken = jnp.sum(taken.astype(wide), axis=0)
    bias_sum = taken[2 * lines :].reshape(2, 2, width)
    grad_ev = with_partner(transposed_dot(x0, back_one))
    second_gate = cross_dot(second_rank, whole_su) + bias[1][None, :]
    grad_inputs = (
        masked * second_gate + layer_grad * first_gate + layer_grad + cross_dot(back_one, full_v)
    ).astype(low)
    return (
        grad_inputs,
        grad_eu,
        grad_ev,
        taken[:lines].astype(low),
        taken[lines : 2 * lines].astype(low),
        bias_sum[0] + bias_sum[1],
    )


def solution(mesh):
    placed = (
        P("dom", "feat"),
        P("dom", "feat"),
        P("dom"),
        P("feat", "dom"),
        P("feat", "dom"),
        P(("feat", "dom"), None),
        P(("feat", "dom"), None),
        P(None, "feat"),
    )
    return jax.shard_map(
        local,
        mesh=mesh,
        in_specs=placed,
        out_specs=(
            P("dom", "feat"),
            P("feat", "dom"),
            P("feat", "dom"),
            P(("feat", "dom"), None),
            P(("feat", "dom"), None),
            P(None, "feat"),
        ),
        check_vma=False,
    )
```

```python
import functools

import jax
import jax.numpy as jnp
from jax import lax
from jax.experimental import pallas as pl
from jax.experimental.pallas import tpu as pltpu
from jax.sharding import PartitionSpec as P

FAR = 2
CHUNK = 256
PARAMS = pltpu.CompilerParams(vmem_limit_bytes=32 * 1024 * 1024)


def core_swap(value):
    pairs = [(source, source ^ 1) for source in range(lax.axis_size("dom"))]
    return lax.ppermute(value, "dom", pairs)


def near_groups():
    half = lax.axis_size("feat") // FAR
    return [[far * half + 2 * pair + bit for far in range(FAR) for bit in range(2)] for pair in range(half // 2)]


def ring_groups():
    half = lax.axis_size("feat") // FAR
    return [[far * half + 2 * step + bit for step in range(half // 2)] for far in range(FAR) for bit in range(2)]


def chip_groups():
    return [list(range(core, lax.axis_size("dom"), 2)) for core in range(2)]


def exchange(value, axis, groups):
    return lax.all_to_all(value, axis, 0, 0, axis_index_groups=groups, tiled=True)


def gathered(value, axis, groups):
    members = len(groups[0])
    repeated = jnp.broadcast_to(value[None], (members, *value.shape))
    return exchange(repeated.reshape(members * value.shape[0], value.shape[1]), axis, groups)


def summed(value, axis, groups):
    pieces = exchange(value, axis, groups).reshape(len(groups[0]), -1, value.shape[1])
    return jnp.sum(pieces.astype(jnp.float32), axis=0).astype(jnp.bfloat16)


def dot(left_side, right_side):
    return jnp.dot(left_side, right_side, preferred_element_type=jnp.float32)


def transposed_dot(left_side, right_side):
    return lax.dot_general(
        left_side, right_side, (((0,), (0,)), ((), ())), preferred_element_type=jnp.float32
    )


def cross_dot(left_side, right_side):
    return lax.dot_general(
        left_side, right_side, (((1,), (1,)), ((), ())), preferred_element_type=jnp.float32
    )


def middle_kernel(sums, x0, masked, own_u, other_u, map_v, bias, both, layer_one, first_adj, kept, bias_sum, total):
    low, wide = jnp.bfloat16, jnp.float32
    rows, half_rank = x0.shape[0], own_u.shape[1]
    step = pl.program_id(0)

    @pl.when(step == 0)
    def _():
        total[...] = jnp.zeros_like(total)

    inputs = x0[...].astype(wide)
    first_gate = (
        cross_dot(sums[:rows, :half_rank], own_u[...])
        + cross_dot(sums[:rows, half_rank:], other_u[...])
        + bias[:1, :]
    )
    layer = (inputs * first_gate + inputs).astype(low)
    layer_grad = masked[...].astype(wide) + cross_dot(sums[rows:, :], map_v[...])
    adj = (layer_grad * inputs).astype(low)
    layer_one[...] = layer
    first_adj[...] = adj
    kept[...] = layer_grad * (first_gate + 1.0)
    bias_sum[...] = jnp.sum(adj.astype(wide), axis=0, keepdims=True)
    total[:rows, :] += dot(layer, map_v[...])
    total[rows:, :half_rank] += dot(adj, own_u[...])
    total[rows:, half_rank:] += dot(adj, other_u[...])

    @pl.when(step == pl.num_programs(0) - 1)
    def _():
        both[...] = total[...].astype(low)


def middle(sums, x0, masked, own_u, other_u, map_v, bias):
    low, wide = jnp.bfloat16, jnp.float32
    rows, width = x0.shape
    rank = sums.shape[1]
    across = pl.BlockSpec((rows, CHUNK), lambda i: (0, i))
    half = pl.BlockSpec((CHUNK, rank // 2), lambda i: (i, 0))
    fixed = pl.BlockSpec((2 * rows, rank), lambda i: (0, 0))
    return pl.pallas_call(
        middle_kernel,
        grid=(width // CHUNK,),
        in_specs=[
            fixed,
            across,
            across,
            half,
            half,
            pl.BlockSpec((CHUNK, rank), lambda i: (i, 0)),
            pl.BlockSpec((2, CHUNK), lambda i: (0, i)),
        ],
        out_specs=[fixed, across, across, across, pl.BlockSpec((1, CHUNK), lambda i: (0, i))],
        out_shape=[
            jax.ShapeDtypeStruct((2 * rows, rank), low),
            jax.ShapeDtypeStruct((rows, width), low),
            jax.ShapeDtypeStruct((rows, width), low),
            jax.ShapeDtypeStruct((rows, width), wide),
            jax.ShapeDtypeStruct((1, width), wide),
        ],
        scratch_shapes=[pltpu.VMEM((2 * rows, rank), wide)],
        compiler_params=PARAMS,
    )(sums, x0, masked, own_u, other_u, map_v, bias)


def split_rows(core, term, keep, give):
    lines = keep.shape[1]
    for pair in range(keep.shape[0]):
        first = term[2 * pair * lines : (2 * pair + 1) * lines]
        second = term[(2 * pair + 1) * lines : (2 * pair + 2) * lines]
        keep[pair] = jnp.where(core == 0, first, second)
        give[pair] = jnp.where(core == 0, second, first).astype(give.dtype)


def early_kernel(place, first_adj, layer_one, sums, keep_u, give_u, keep_v, give_v):
    rows, half_rank = first_adj.shape[0], keep_u.shape[1]
    keep_u[...] = transposed_dot(first_adj[...], sums[:rows, :half_rank])
    give_u[...] = transposed_dot(first_adj[...], sums[:rows, half_rank:]).astype(give_u.dtype)
    split_rows(place[0], transposed_dot(layer_one[...], sums[rows:, :]), keep_v, give_v)


def late_kernel(place, second_adj, sums, keep, give):
    rows = second_adj.shape[0]
    split_rows(place[0], transposed_dot(second_adj[...], sums[:rows, :]), keep, give)


def terms(kernel, core, acts, sums, lines, with_expert):
    low, wide = jnp.bfloat16, jnp.float32
    rows, width = acts[0].shape
    rank = sums.shape[1]
    pairs = CHUNK // (2 * lines)
    expert = pl.BlockSpec((CHUNK, rank // 2), lambda i, place: (i, 0))
    shared = pl.BlockSpec((pairs, lines, rank), lambda i, place: (i, 0, 0))
    whole_expert, whole_shared = (width, rank // 2), (width // (2 * lines), lines, rank)
    specs = ([expert] * 2 if with_expert else []) + [shared] * 2
    shapes = ([whole_expert] * 2 if with_expert else []) + [whole_shared] * 2
    return pl.pallas_call(
        kernel,
        grid_spec=pltpu.PrefetchScalarGridSpec(
            num_scalar_prefetch=1,
            grid=(width // CHUNK,),
            in_specs=[pl.BlockSpec((rows, CHUNK), lambda i, place: (0, i))] * len(acts)
            + [pl.BlockSpec(sums.shape, lambda i, place: (0, 0))],
            out_specs=specs,
        ),
        out_shape=[jax.ShapeDtypeStruct(shape, (wide, low)[i % 2]) for i, shape in enumerate(shapes)],
        compiler_params=PARAMS,
    )(core[None], *acts, sums)


def last_kernel(lines, taken, grad_su, grad_sv, grad_bias):
    low, wide = jnp.bfloat16, jnp.float32
    total = jnp.sum(taken[...].astype(wide), axis=0)
    grad_su[...] = total[:lines].astype(low)
    grad_sv[...] = total[lines : 2 * lines].astype(low)
    sums = total[2 * lines :]
    half = sums.shape[0] // 2
    sums = sums[:half] + sums[half:]
    rank = sums.shape[1]
    per_row = half // 2
    for i in range(half):
        column = (i % per_row) * rank
        grad_bias[i // per_row : i // per_row + 1, column : column + rank] = sums[i : i + 1]


def last_sum(taken, lines, width):
    rank = taken.shape[2]
    return pl.pallas_call(
        functools.partial(last_kernel, lines),
        out_shape=[
            jax.ShapeDtypeStruct((lines, rank), jnp.bfloat16),
            jax.ShapeDtypeStruct((lines, rank), jnp.bfloat16),
            jax.ShapeDtypeStruct((2, width), jnp.float32),
        ],
        compiler_params=PARAMS,
    )(taken)


def local(x0, cotangent, domain_ids, expert_u, expert_v, shared_u, shared_v, bias):
    low = jnp.bfloat16
    wide = jnp.float32
    rows, width = x0.shape
    half_rank = expert_u.shape[1]
    rank = 2 * half_rank
    chips = lax.axis_size("dom") // 2
    lines = shared_u.shape[0]
    domain = lax.axis_index("dom") // 2
    core = lax.axis_index("dom") % 2

    own_maps = gathered(jnp.concatenate([shared_u, shared_v], 0), "dom", chip_groups())
    own_maps = own_maps.reshape(chips, 2, lines, rank)
    other_v = core_swap(expert_v)
    full_v = jnp.concatenate([expert_v, other_v], 1)

    def whole(own, other):
        pair = [jnp.where(core == 0, own, other), jnp.where(core == 0, other, own)]
        return jnp.stack(pair, 1).reshape(width, rank)

    masked = jnp.where((domain_ids == domain)[:, None], cotangent, jnp.zeros_like(cotangent))
    second_adj = (masked.astype(wide) * x0.astype(wide)).astype(low)
    bias_two = jnp.sum(second_adj.astype(wide), axis=0, keepdims=True)

    first_part = dot(x0, full_v).astype(low)
    whole_su = whole(own_maps[:, 0], core_swap(own_maps[:, 0]))
    back_two_part = dot(second_adj, whole_su).astype(low)
    both = jnp.concatenate([first_part, back_two_part], 0)
    own_sv, expert_u, both = lax.optimization_barrier((own_maps[:, 1], expert_u, both))
    near, ring = near_groups(), ring_groups()
    part = summed(summed(both, "feat", near), "feat", ring)
    whole_sv = whole(own_sv, core_swap(own_sv))
    other_u = core_swap(expert_u)
    part, whole_sv, other_u, masked = lax.optimization_barrier((part, whole_sv, other_u, masked))
    sums = gathered(gathered(part, "feat", ring), "feat", near)

    both, layer_one, first_adj, kept, bias_one = middle(sums, x0, masked, expert_u, other_u, whole_sv, bias)
    part = summed(both, "feat", near)
    part, sums, first_adj, layer_one = lax.optimization_barrier((part, sums, first_adj, layer_one))
    keep_eu, give_eu, keep_sv, give_sv = terms(early_kernel, core, [first_adj, layer_one], sums, lines, True)
    part = summed(part, "feat", ring)
    peer_eu, peer_sv = core_swap(give_eu), core_swap(give_sv)
    bias_terms = jnp.concatenate([bias_one, bias_two], 0)
    bias_terms = bias_terms + core_swap(bias_terms)
    part, peer_eu, peer_sv, bias_terms = lax.optimization_barrier((part, peer_eu, peer_sv, bias_terms))
    part = gathered(part, "feat", ring)
    bias_high = bias_terms.astype(low)
    bias_rest = (bias_terms - bias_high.astype(wide)).astype(low)
    bias_lines = jnp.stack([bias_high, bias_rest]).reshape(4 * width // rank, rank)
    bias_lines = jnp.broadcast_to(bias_lines[None], (chips, *bias_lines.shape))
    grad_eu = (keep_eu + peer_eu.astype(wide)).astype(low)
    part_sv = (keep_sv + peer_sv.astype(wide)).astype(low)
    sent = jnp.concatenate([jnp.zeros_like(part_sv), part_sv, bias_lines], 1)
    part, sent, grad_eu = lax.optimization_barrier((part, sent, grad_eu))
    sums = gathered(part, "feat", near)

    keep_su, give_su = terms(late_kernel, core, [second_adj], sums, lines, False)
    part_su = (keep_su + core_swap(give_su).astype(wide)).astype(low)
    sent = lax.dynamic_update_slice(sent, part_su, (0, 0, 0))
    sent, sums = lax.optimization_barrier((sent, sums))
    taken = exchange(sent.reshape(-1, rank), "dom", chip_groups()).reshape(sent.shape)
    second_rank, back_one = sums[:rows], sums[rows:]
    partial_ev = transposed_dot(x0, back_one)
    peer_ev = core_swap(partial_ev[:, half_rank:].astype(low))
    grad_ev = (partial_ev[:, :half_rank] + peer_ev.astype(wide)).astype(low)
    second_gate = cross_dot(second_rank, whole_su) + bias[1][None, :]
    grad_inputs = (masked.astype(wide) * second_gate + kept + cross_dot(back_one, full_v)).astype(low)
    grad_su, grad_sv, grad_bias = last_sum(taken, lines, width)
    return (grad_inputs, grad_eu, grad_ev, grad_su, grad_sv, grad_bias)


def solution(mesh):
    placed = (
        P("dom", "feat"),
        P("dom", "feat"),
        P("dom"),
        P("feat", "dom"),
        P("feat", "dom"),
        P(("feat", "dom"), None),
        P(("feat", "dom"), None),
        P(None, "feat"),
    )
    return jax.shard_map(
        local,
        mesh=mesh,
        in_specs=placed,
        out_specs=(
            P("dom", "feat"),
            P("feat", "dom"),
            P("feat", "dom"),
            P(("feat", "dom"), None),
            P(("feat", "dom"), None),
            P(None, "feat"),
        ),
        check_vma=False,
    )
```

```python
import functools

import jax
import jax.numpy as jnp
from jax import lax
from jax.experimental import pallas as pl
from jax.experimental.pallas import tpu as pltpu
from jax.sharding import PartitionSpec as P

FAR = 2
CHUNK = 256
SPARE = 16
PARAMS = pltpu.CompilerParams(vmem_limit_bytes=32 * 1024 * 1024)


def dom_swap(value, bit):
    pairs = [(source, source ^ 2**bit) for source in range(lax.axis_size("dom"))]
    return lax.ppermute(value, "dom", pairs)


def core_swap(value):
    return dom_swap(value, 0)


def joined(value, bit):
    other = dom_swap(value, bit)
    low_side = (lax.axis_index("dom") // 2**bit) % 2 == 0
    return jnp.where(low_side, jnp.concatenate([value, other], 0), jnp.concatenate([other, value], 0))


def near_groups():
    half = lax.axis_size("feat") // FAR
    return [[far * half + 2 * pair + bit for far in range(FAR) for bit in range(2)] for pair in range(half // 2)]


def ring_groups():
    half = lax.axis_size("feat") // FAR
    return [[far * half + 2 * step + bit for step in range(half // 2)] for far in range(FAR) for bit in range(2)]


def chip_groups():
    return [list(range(core, lax.axis_size("dom"), 2)) for core in range(2)]


def exchange(value, axis, groups):
    return lax.all_to_all(value, axis, 0, 0, axis_index_groups=groups, tiled=True)


def gathered(value, axis, groups):
    members = len(groups[0])
    repeated = jnp.broadcast_to(value[None], (members, *value.shape))
    return exchange(repeated.reshape(members * value.shape[0], value.shape[1]), axis, groups)


def summed(value, axis, groups):
    pieces = exchange(value, axis, groups).reshape(len(groups[0]), -1, value.shape[1])
    return jnp.sum(pieces.astype(jnp.float32), axis=0).astype(jnp.bfloat16)


def dot(left_side, right_side):
    return jnp.dot(left_side, right_side, preferred_element_type=jnp.float32)


def transposed_dot(left_side, right_side):
    return lax.dot_general(
        left_side, right_side, (((0,), (0,)), ((), ())), preferred_element_type=jnp.float32
    )


def cross_dot(left_side, right_side):
    return lax.dot_general(
        left_side, right_side, (((1,), (1,)), ((), ())), preferred_element_type=jnp.float32
    )


def in_hbm(value):
    return pltpu.with_memory_space_constraint(value, pltpu.HBM)


def middle_kernel(sums, x0, masked, own_u, other_u, map_v, bias, both, layer_one, first_adj, kept, bias_sum, total):
    low, wide = jnp.bfloat16, jnp.float32
    rows, half_rank = x0.shape[0], own_u.shape[1]
    step = pl.program_id(0)

    @pl.when(step == 0)
    def _():
        total[...] = jnp.zeros_like(total)

    inputs = x0[...].astype(wide)
    first_gate = (
        cross_dot(sums[:rows, :half_rank], own_u[...])
        + cross_dot(sums[:rows, half_rank:], other_u[...])
        + bias[:1, :]
    )
    layer = (inputs * first_gate + inputs).astype(low)
    layer_grad = masked[...].astype(wide) + cross_dot(sums[rows:, :], map_v[...])
    adj = (layer_grad * inputs).astype(low)
    layer_one[...] = layer
    first_adj[...] = adj
    kept[...] = layer_grad * (first_gate + 1.0)
    bias_sum[...] = jnp.sum(adj.astype(wide), axis=0, keepdims=True)
    total[:rows, :] += dot(layer, map_v[...])
    total[rows:, :half_rank] += dot(adj, own_u[...])
    total[rows:, half_rank:] += dot(adj, other_u[...])

    @pl.when(step == pl.num_programs(0) - 1)
    def _():
        both[...] = total[...].astype(low)


def middle(sums, x0, masked, own_u, other_u, map_v, bias):
    low, wide = jnp.bfloat16, jnp.float32
    rows, width = x0.shape
    rank = sums.shape[1]
    across = pl.BlockSpec((rows, CHUNK), lambda i: (0, i))
    half = pl.BlockSpec((CHUNK, rank // 2), lambda i: (i, 0))
    fixed = pl.BlockSpec((2 * rows, rank), lambda i: (0, 0))
    return pl.pallas_call(
        middle_kernel,
        grid=(width // CHUNK,),
        in_specs=[
            fixed,
            across,
            across,
            half,
            half,
            pl.BlockSpec((CHUNK, rank), lambda i: (i, 0)),
            pl.BlockSpec((2, CHUNK), lambda i: (0, i)),
        ],
        out_specs=[fixed, across, across, across, pl.BlockSpec((1, CHUNK), lambda i: (0, i))],
        out_shape=[
            jax.ShapeDtypeStruct((2 * rows, rank), low),
            pltpu.HBM((rows, width), low),
            pltpu.HBM((rows, width), low),
            pltpu.HBM((rows, width), wide),
            jax.ShapeDtypeStruct((1, width), wide),
        ],
        scratch_shapes=[pltpu.VMEM((2 * rows, rank), wide)],
        compiler_params=PARAMS,
    )(sums, x0, masked, own_u, other_u, map_v, bias)


def halves_of(term, core, pair, lines):
    first = term[2 * pair * lines : (2 * pair + 1) * lines]
    second = term[(2 * pair + 1) * lines : (2 * pair + 2) * lines]
    return jnp.where(core == 0, first, second), jnp.where(core == 0, second, first)


def in_two(line):
    high = line.astype(jnp.bfloat16).astype(jnp.float32)
    return high, (line - high).astype(jnp.bfloat16).astype(jnp.float32)


def early_kernel(place, first_adj, layer_one, sums, bias_one, bias_two, keep_u, keep_v, give):
    low = give.dtype
    rows, half_rank = first_adj.shape[0], keep_u.shape[1]
    pairs, lines, _ = keep_v.shape
    keep_u[...] = transposed_dot(first_adj[...], sums[:rows, :half_rank])
    give[0, :CHUNK, :half_rank] = transposed_dot(first_adj[...], sums[:rows, half_rank:]).astype(low)
    term = transposed_dot(layer_one[...], sums[rows:, :])
    for pair in range(pairs):
        keep_v[pair], away = halves_of(term, place[0], pair, lines)
        top = 2 * pair * lines
        give[0, top : top + lines, half_rank:] = away[:, :half_rank].astype(low)
        give[0, top + lines : top + 2 * lines, half_rank:] = away[:, half_rank:].astype(low)
    one = jnp.concatenate(in_two(bias_one[...]), 1)
    two = jnp.concatenate(in_two(bias_two[...]), 1)
    row = lax.broadcasted_iota(jnp.int32, (SPARE, one.shape[1]), 0)
    give[0, CHUNK:, :] = jnp.where(row == 0, one, jnp.where(row == 1, two, 0.0)).astype(low)


def early_terms(core, first_adj, layer_one, sums, bias_one, bias_two, lines):
    low, wide = jnp.bfloat16, jnp.float32
    rows, width = first_adj.shape
    rank = sums.shape[1]
    pairs = CHUNK // (2 * lines)
    chunks = width // CHUNK
    across = pl.BlockSpec((rows, CHUNK), lambda i, place: (0, i))
    line = pl.BlockSpec((1, CHUNK), lambda i, place: (0, i))
    return pl.pallas_call(
        early_kernel,
        grid_spec=pltpu.PrefetchScalarGridSpec(
            num_scalar_prefetch=1,
            grid=(chunks,),
            in_specs=[across, across, pl.BlockSpec(sums.shape, lambda i, place: (0, 0)), line, line],
            out_specs=[
                pl.BlockSpec((CHUNK, rank // 2), lambda i, place: (i, 0)),
                pl.BlockSpec((pairs, lines, rank), lambda i, place: (i, 0, 0)),
                pl.BlockSpec((1, CHUNK + SPARE, rank), lambda i, place: (i, 0, 0)),
            ],
        ),
        out_shape=[
            pltpu.HBM((width, rank // 2), wide),
            pltpu.HBM((width // (2 * lines), lines, rank), wide),
            pltpu.HBM((chunks, CHUNK + SPARE, rank), low),
        ],
        compiler_params=PARAMS,
    )(core[None], in_hbm(first_adj), in_hbm(layer_one), sums, bias_one, bias_two)


def finish_kernel(keep_u, keep_v, peer, bias_one, bias_two, grad_eu, sent):
    low, wide = sent.dtype, jnp.float32
    half_rank = grad_eu.shape[1]
    chips, lines, _ = keep_v.shape
    chunks = peer.shape[0]
    pairs = chips // chunks
    tail = jnp.zeros((SPARE, 2 * half_rank), wide)
    row = lax.broadcasted_iota(jnp.int32, tail.shape, 0)
    for i in range(chunks):
        spot = slice(i * CHUNK, (i + 1) * CHUNK)
        grad_eu[spot, :] = (keep_u[spot, :] + peer[i, :CHUNK, :half_rank].astype(wide)).astype(low)
        for pair in range(pairs):
            top = 2 * pair * lines
            left = peer[i, top : top + lines, half_rank:].astype(wide)
            right = peer[i, top + lines : top + 2 * lines, half_rank:].astype(wide)
            chip = i * pairs + pair
            sent[chip, :lines, :] = jnp.zeros((lines, 2 * half_rank), low)
            sent[chip, lines : 2 * lines, :half_rank] = (keep_v[chip, :, :half_rank] + left).astype(low)
            sent[chip, lines : 2 * lines, half_rank:] = (keep_v[chip, :, half_rank:] + right).astype(low)
        theirs = peer[i, CHUNK:, :].astype(wide)
        theirs = theirs[:, :half_rank] + theirs[:, half_rank:]
        for t, bias in enumerate((bias_one, bias_two)):
            high, rest = in_two(bias[:, spot])
            line = jnp.concatenate(in_two((high + rest) + theirs[t : t + 1]), 1)
            tail = jnp.where(row == 2 * i + t, line, tail)
    for chip in range(chips):
        sent[chip, 2 * lines :, :] = tail.astype(low)


def finished(keep_u, keep_v, peer, bias_one, bias_two):
    low = jnp.bfloat16
    chips, lines, rank = keep_v.shape
    return pl.pallas_call(
        finish_kernel,
        out_shape=[
            jax.ShapeDtypeStruct(keep_u.shape, low),
            jax.ShapeDtypeStruct((chips, 2 * lines + SPARE, rank), low),
        ],
        compiler_params=PARAMS,
    )(keep_u, keep_v, peer, bias_one, bias_two)


def late_kernel(place, second_adj, sums, keep, give):
    rows = second_adj.shape[0]
    pairs, lines, _ = keep.shape
    term = transposed_dot(second_adj[...], sums[:rows, :])
    for pair in range(pairs):
        keep[pair], away = halves_of(term, place[0], pair, lines)
        give[pair] = away.astype(give.dtype)


def late_terms(core, second_adj, sums, lines):
    rows, width = second_adj.shape
    rank = sums.shape[1]
    shared = pl.BlockSpec((CHUNK // (2 * lines), lines, rank), lambda i, place: (i, 0, 0))
    shape = (width // (2 * lines), lines, rank)
    return pl.pallas_call(
        late_kernel,
        grid_spec=pltpu.PrefetchScalarGridSpec(
            num_scalar_prefetch=1,
            grid=(width // CHUNK,),
            in_specs=[
                pl.BlockSpec((rows, CHUNK), lambda i, place: (0, i)),
                pl.BlockSpec(sums.shape, lambda i, place: (0, 0)),
            ],
            out_specs=[shared, shared],
        ),
        out_shape=[jax.ShapeDtypeStruct(shape, jnp.float32), jax.ShapeDtypeStruct(shape, jnp.bfloat16)],
        compiler_params=PARAMS,
    )(core[None], second_adj, sums)


def last_kernel(lines, taken, grad_su, grad_sv, grad_bias):
    low, wide = jnp.bfloat16, jnp.float32
    total = jnp.sum(taken[...].astype(wide), axis=0)
    grad_su[...] = total[:lines].astype(low)
    grad_sv[...] = total[lines : 2 * lines].astype(low)
    sums = total[2 * lines :]
    sums = sums[:, : sums.shape[1] // 2] + sums[:, sums.shape[1] // 2 :]
    for i in range(grad_bias.shape[1] // CHUNK):
        grad_bias[:, i * CHUNK : (i + 1) * CHUNK] = sums[2 * i : 2 * i + 2]


def last_sum(taken, lines, width):
    rank = taken.shape[2]
    return pl.pallas_call(
        functools.partial(last_kernel, lines),
        out_shape=[
            jax.ShapeDtypeStruct((lines, rank), jnp.bfloat16),
            jax.ShapeDtypeStruct((lines, rank), jnp.bfloat16),
            jax.ShapeDtypeStruct((2, width), jnp.float32),
        ],
        compiler_params=PARAMS,
    )(taken)


def local(x0, cotangent, domain_ids, expert_u, expert_v, shared_u, shared_v, bias):
    low = jnp.bfloat16
    wide = jnp.float32
    rows, width = x0.shape
    half_rank = expert_u.shape[1]
    rank = 2 * half_rank
    chips = lax.axis_size("dom") // 2
    lines = shared_u.shape[0]
    domain = lax.axis_index("dom") // 2
    core = lax.axis_index("dom") % 2

    own_su = gathered(shared_u, "dom", chip_groups()).reshape(chips, lines, rank)
    other_v = core_swap(expert_v)
    full_v = jnp.concatenate([expert_v, other_v], 1)

    def whole(own, other):
        pair = [jnp.where(core == 0, own, other), jnp.where(core == 0, other, own)]
        return jnp.stack(pair, 1).reshape(width, rank)

    masked = jnp.where((domain_ids == domain)[:, None], cotangent, jnp.zeros_like(cotangent))
    second_adj = (masked.astype(wide) * x0.astype(wide)).astype(low)
    bias_two = jnp.sum(second_adj.astype(wide), axis=0, keepdims=True)

    first_part = dot(x0, full_v).astype(low)
    whole_su = whole(own_su, core_swap(own_su))
    back_two_part = dot(second_adj, whole_su).astype(low)
    both = jnp.concatenate([first_part, back_two_part], 0)
    near, ring = near_groups(), ring_groups()
    shared_v, both = lax.optimization_barrier((shared_v, both))
    whole_sv = joined(shared_v, 0)
    part = summed(both, "feat", near)
    part, whole_sv = lax.optimization_barrier((part, whole_sv))
    whole_sv = joined(joined(whole_sv, 1), 2)
    part = summed(part, "feat", ring)
    part, whole_sv, expert_u = lax.optimization_barrier((part, whole_sv, expert_u))
    whole_sv = joined(whole_sv, 3)
    other_u = core_swap(expert_u)
    part = gathered(part, "feat", ring)
    part, whole_sv, other_u, masked = lax.optimization_barrier((part, whole_sv, other_u, masked))
    sums = gathered(part, "feat", near)

    both, layer_one, first_adj, kept, bias_one = middle(sums, x0, masked, expert_u, other_u, whole_sv, bias)
    keep_eu, keep_sv, give = early_terms(core, first_adj, layer_one, sums, bias_one, bias_two, lines)
    part = summed(both, "feat", near)
    part, give = lax.optimization_barrier((part, give))
    part = summed(part, "feat", ring)
    part, peer = lax.optimization_barrier((part, core_swap(give)))
    grad_eu, sent = finished(keep_eu, keep_sv, peer, bias_one, bias_two)
    part = gathered(part, "feat", ring)
    part, sent, grad_eu = lax.optimization_barrier((part, sent, grad_eu))
    sums = gathered(part, "feat", near)

    keep_su, give_su = late_terms(core, second_adj, sums, lines)
    part_su = (keep_su + core_swap(give_su).astype(wide)).astype(low)
    sent = lax.dynamic_update_slice(sent, part_su, (0, 0, 0))
    sent, sums = lax.optimization_barrier((sent, sums))
    taken = exchange(sent.reshape(-1, rank), "dom", chip_groups()).reshape(sent.shape)
    second_rank, back_one = sums[:rows], sums[rows:]
    partial_ev = transposed_dot(x0, back_one)
    peer_ev = core_swap(partial_ev[:, half_rank:].astype(low))
    grad_ev = (partial_ev[:, :half_rank] + peer_ev.astype(wide)).astype(low)
    second_gate = cross_dot(second_rank, whole_su) + bias[1][None, :]
    grad_inputs = (masked.astype(wide) * second_gate + kept + cross_dot(back_one, full_v)).astype(low)
    grad_su, grad_sv, grad_bias = last_sum(taken, lines, width)
    return (grad_inputs, grad_eu, grad_ev, grad_su, grad_sv, grad_bias)


def solution(mesh):
    placed = (
        P("dom", "feat"),
        P("dom", "feat"),
        P("dom"),
        P("feat", "dom"),
        P("feat", "dom"),
        P(("feat", "dom"), None),
        P(("feat", "dom"), None),
        P(None, "feat"),
    )
    return jax.shard_map(
        local,
        mesh=mesh,
        in_specs=placed,
        out_specs=(
            P("dom", "feat"),
            P("feat", "dom"),
            P("feat", "dom"),
            P(("feat", "dom"), None),
            P(("feat", "dom"), None),
            P(None, "feat"),
        ),
        check_vma=False,
    )
```

```python
import functools

import jax
import jax.numpy as jnp
from jax import lax
from jax.experimental import pallas as pl
from jax.experimental.pallas import tpu as pltpu
from jax.sharding import PartitionSpec as P

FAR = 2
CHUNK = 256
SPARE = 16
PARAMS = pltpu.CompilerParams(vmem_limit_bytes=32 * 1024 * 1024)


def dom_swap(value, bit):
    pairs = [(source, source ^ 2**bit) for source in range(lax.axis_size("dom"))]
    return lax.ppermute(value, "dom", pairs)


def core_swap(value):
    return dom_swap(value, 0)


def joined(value, bit, axis):
    other = dom_swap(value, bit)
    low_side = (lax.axis_index("dom") // 2**bit) % 2 == 0
    pair = [jnp.where(low_side, value, other), jnp.where(low_side, other, value)]
    return jnp.stack(pair, axis)


def near_groups():
    half = lax.axis_size("feat") // FAR
    return [[far * half + 2 * pair + bit for far in range(FAR) for bit in range(2)] for pair in range(half // 2)]


def ring_groups():
    half = lax.axis_size("feat") // FAR
    return [[far * half + 2 * step + bit for step in range(half // 2)] for far in range(FAR) for bit in range(2)]


def chip_groups():
    return [list(range(core, lax.axis_size("dom"), 2)) for core in range(2)]


def exchange(value, axis, groups):
    return lax.all_to_all(value, axis, 0, 0, axis_index_groups=groups, tiled=True)


def gathered(value, axis, groups):
    members = len(groups[0])
    repeated = jnp.broadcast_to(value[None], (members, *value.shape))
    return exchange(repeated.reshape(members * value.shape[0], value.shape[1]), axis, groups)


def summed(value, axis, groups):
    pieces = exchange(value, axis, groups).reshape(len(groups[0]), -1, value.shape[1])
    return jnp.sum(pieces.astype(jnp.float32), axis=0).astype(jnp.bfloat16)


def dot(left_side, right_side):
    return jnp.dot(left_side, right_side, preferred_element_type=jnp.float32)


def transposed_dot(left_side, right_side):
    return lax.dot_general(
        left_side, right_side, (((0,), (0,)), ((), ())), preferred_element_type=jnp.float32
    )


def cross_dot(left_side, right_side):
    return lax.dot_general(
        left_side, right_side, (((1,), (1,)), ((), ())), preferred_element_type=jnp.float32
    )


def in_hbm(value):
    return pltpu.with_memory_space_constraint(value, pltpu.HBM)


def middle_kernel(sums, x0, masked, own_u, other_u, map_v, bias, both, layer_one, first_adj, kept, bias_sum, total):
    low, wide = jnp.bfloat16, jnp.float32
    rows, half_rank = x0.shape[0], own_u.shape[1]
    step = pl.program_id(0)

    @pl.when(step == 0)
    def _():
        total[...] = jnp.zeros_like(total)

    inputs = x0[...].astype(wide)
    first_gate = (
        cross_dot(sums[:rows, :half_rank], own_u[...])
        + cross_dot(sums[:rows, half_rank:], other_u[...])
        + bias[:1, :]
    )
    layer = (inputs * first_gate + inputs).astype(low)
    layer_grad = masked[...].astype(wide) + cross_dot(sums[rows:, :], map_v[...])
    adj = (layer_grad * inputs).astype(low)
    layer_one[...] = layer
    first_adj[...] = adj
    kept[...] = layer_grad * (first_gate + 1.0)
    bias_sum[...] = jnp.sum(adj.astype(wide), axis=0, keepdims=True)
    total[:rows, :] += dot(layer, map_v[...])
    total[rows:, :half_rank] += dot(adj, own_u[...])
    total[rows:, half_rank:] += dot(adj, other_u[...])

    @pl.when(step == pl.num_programs(0) - 1)
    def _():
        both[...] = total[...].astype(low)


def middle(sums, x0, masked, own_u, other_u, map_v, bias):
    low, wide = jnp.bfloat16, jnp.float32
    rows, width = x0.shape
    rank = sums.shape[1]
    across = pl.BlockSpec((rows, CHUNK), lambda i: (0, i))
    half = pl.BlockSpec((CHUNK, rank // 2), lambda i: (i, 0))
    fixed = pl.BlockSpec((2 * rows, rank), lambda i: (0, 0))
    return pl.pallas_call(
        middle_kernel,
        grid=(width // CHUNK,),
        in_specs=[
            fixed,
            across,
            across,
            half,
            half,
            pl.BlockSpec((CHUNK, rank), lambda i: (i, 0)),
            pl.BlockSpec((2, CHUNK), lambda i: (0, i)),
        ],
        out_specs=[fixed, across, across, across, pl.BlockSpec((1, CHUNK), lambda i: (0, i))],
        out_shape=[
            pltpu.HBM((2 * rows, rank), low),
            pltpu.HBM((rows, width), low),
            pltpu.HBM((rows, width), low),
            pltpu.HBM((rows, width), wide),
            jax.ShapeDtypeStruct((1, width), wide),
        ],
        scratch_shapes=[pltpu.VMEM((2 * rows, rank), wide)],
        compiler_params=PARAMS,
    )(sums, *map(in_hbm, (x0, masked, own_u, other_u, map_v)), bias)


def halves_of(term, core, pair, lines):
    first = term[2 * pair * lines : (2 * pair + 1) * lines]
    second = term[(2 * pair + 1) * lines : (2 * pair + 2) * lines]
    return jnp.where(core == 0, first, second), jnp.where(core == 0, second, first)


def in_two(line):
    high = line.astype(jnp.bfloat16).astype(jnp.float32)
    return high, (line - high).astype(jnp.bfloat16).astype(jnp.float32)


def early_kernel(place, first_adj, layer_one, sums, bias_one, bias_two, keep_u, keep_v, give):
    low = give.dtype
    rows, half_rank = first_adj.shape[0], keep_u.shape[1]
    pairs, lines, _ = keep_v.shape
    keep_u[...] = transposed_dot(first_adj[...], sums[:rows, :half_rank])
    give[0, :CHUNK, :half_rank] = transposed_dot(first_adj[...], sums[:rows, half_rank:]).astype(low)
    term = transposed_dot(layer_one[...], sums[rows:, :])
    for pair in range(pairs):
        keep_v[pair], away = halves_of(term, place[0], pair, lines)
        top = 2 * pair * lines
        give[0, top : top + lines, half_rank:] = away[:, :half_rank].astype(low)
        give[0, top + lines : top + 2 * lines, half_rank:] = away[:, half_rank:].astype(low)
    one = jnp.concatenate(in_two(bias_one[...]), 1)
    two = jnp.concatenate(in_two(bias_two[...]), 1)
    row = lax.broadcasted_iota(jnp.int32, (SPARE, one.shape[1]), 0)
    give[0, CHUNK:, :] = jnp.where(row == 0, one, jnp.where(row == 1, two, 0.0)).astype(low)


def early_terms(core, first_adj, layer_one, sums, bias_one, bias_two, lines):
    low, wide = jnp.bfloat16, jnp.float32
    rows, width = first_adj.shape
    rank = sums.shape[1]
    pairs = CHUNK // (2 * lines)
    chunks = width // CHUNK
    across = pl.BlockSpec((rows, CHUNK), lambda i, place: (0, i))
    line = pl.BlockSpec((1, CHUNK), lambda i, place: (0, i))
    return pl.pallas_call(
        early_kernel,
        grid_spec=pltpu.PrefetchScalarGridSpec(
            num_scalar_prefetch=1,
            grid=(chunks,),
            in_specs=[across, across, pl.BlockSpec(sums.shape, lambda i, place: (0, 0)), line, line],
            out_specs=[
                pl.BlockSpec((CHUNK, rank // 2), lambda i, place: (i, 0)),
                pl.BlockSpec((pairs, lines, rank), lambda i, place: (i, 0, 0)),
                pl.BlockSpec((1, CHUNK + SPARE, rank), lambda i, place: (i, 0, 0)),
            ],
        ),
        out_shape=[
            pltpu.HBM((width, rank // 2), wide),
            pltpu.HBM((width // (2 * lines), lines, rank), wide),
            pltpu.HBM((chunks, CHUNK + SPARE, rank), low),
        ],
        compiler_params=PARAMS,
    )(core[None], in_hbm(first_adj), in_hbm(layer_one), sums, bias_one, bias_two)


def finish_kernel(keep_u, give_u, keep_v, peer, bias_one, bias_two, sent):
    low, wide = sent.dtype, jnp.float32
    chips, lines, rank = keep_v.shape
    half_rank = rank // 2
    chunks = peer.shape[0]
    pairs = chips // chunks
    tail = jnp.zeros((SPARE, rank), wide)
    row = lax.broadcasted_iota(jnp.int32, tail.shape, 0)
    for i in range(chunks):
        for pair in range(pairs):
            top = 2 * pair * lines
            left = peer[i, top : top + lines, half_rank:].astype(wide)
            right = peer[i, top + lines : top + 2 * lines, half_rank:].astype(wide)
            chip = i * pairs + pair
            sent[chip, :lines, :] = (keep_u[chip] + give_u[chip].astype(wide)).astype(low)
            sent[chip, lines : 2 * lines, :half_rank] = (keep_v[chip, :, :half_rank] + left).astype(low)
            sent[chip, lines : 2 * lines, half_rank:] = (keep_v[chip, :, half_rank:] + right).astype(low)
        theirs = peer[i, CHUNK:, :].astype(wide)
        theirs = theirs[:, :half_rank] + theirs[:, half_rank:]
        spot = slice(i * CHUNK, (i + 1) * CHUNK)
        for t, bias in enumerate((bias_one, bias_two)):
            high, rest = in_two(bias[:, spot])
            line = jnp.concatenate(in_two((high + rest) + theirs[t : t + 1]), 1)
            tail = jnp.where(row == 2 * i + t, line, tail)
    for chip in range(chips):
        sent[chip, 2 * lines :, :] = tail.astype(low)


def finished(keep_u, peer_u, keep_v, peer, bias_one, bias_two):
    chips, lines, rank = keep_v.shape
    return pl.pallas_call(
        finish_kernel,
        out_shape=jax.ShapeDtypeStruct((chips, 2 * lines + SPARE, rank), jnp.bfloat16),
        compiler_params=PARAMS,
    )(keep_u, peer_u, keep_v, peer, bias_one, bias_two)


def late_kernel(place, second_adj, sums, keep, give):
    rows = second_adj.shape[0]
    pairs, lines, _ = keep.shape
    term = transposed_dot(second_adj[...], sums[:rows, :])
    for pair in range(pairs):
        keep[pair], away = halves_of(term, place[0], pair, lines)
        give[pair] = away.astype(give.dtype)


def late_terms(core, second_adj, sums, lines):
    rows, width = second_adj.shape
    rank = sums.shape[1]
    shared = pl.BlockSpec((CHUNK // (2 * lines), lines, rank), lambda i, place: (i, 0, 0))
    shape = (width // (2 * lines), lines, rank)
    return pl.pallas_call(
        late_kernel,
        grid_spec=pltpu.PrefetchScalarGridSpec(
            num_scalar_prefetch=1,
            grid=(width // CHUNK,),
            in_specs=[
                pl.BlockSpec((rows, CHUNK), lambda i, place: (0, i)),
                pl.BlockSpec(sums.shape, lambda i, place: (0, 0)),
            ],
            out_specs=[shared, shared],
        ),
        out_shape=[jax.ShapeDtypeStruct(shape, jnp.float32), jax.ShapeDtypeStruct(shape, jnp.bfloat16)],
        compiler_params=PARAMS,
    )(core[None], second_adj, sums)


def last_kernel(lines, taken, grad_su, grad_sv, grad_bias):
    low, wide = jnp.bfloat16, jnp.float32
    total = jnp.sum(taken[...].astype(wide), axis=0)
    grad_su[...] = total[:lines].astype(low)
    grad_sv[...] = total[lines : 2 * lines].astype(low)
    sums = total[2 * lines :]
    sums = sums[:, : sums.shape[1] // 2] + sums[:, sums.shape[1] // 2 :]
    for i in range(grad_bias.shape[1] // CHUNK):
        grad_bias[:, i * CHUNK : (i + 1) * CHUNK] = sums[2 * i : 2 * i + 2]


def last_sum(taken, lines, width):
    rank = taken.shape[2]
    return pl.pallas_call(
        functools.partial(last_kernel, lines),
        out_shape=[
            jax.ShapeDtypeStruct((lines, rank), jnp.bfloat16),
            jax.ShapeDtypeStruct((lines, rank), jnp.bfloat16),
            jax.ShapeDtypeStruct((2, width), jnp.float32),
        ],
        compiler_params=PARAMS,
    )(taken)


def local(x0, cotangent, domain_ids, expert_u, expert_v, shared_u, shared_v, bias):
    low = jnp.bfloat16
    wide = jnp.float32
    rows, width = x0.shape
    half_rank = expert_u.shape[1]
    rank = 2 * half_rank
    chips = lax.axis_size("dom") // 2
    lines = shared_u.shape[0]
    domain = lax.axis_index("dom") // 2
    core = lax.axis_index("dom") % 2

    own_su = gathered(shared_u, "dom", chip_groups()).reshape(chips, lines, rank)
    other_v = core_swap(expert_v)
    other_u = core_swap(expert_u)
    full_v = jnp.concatenate([expert_v, other_v], 1)

    masked = jnp.where((domain_ids == domain)[:, None], cotangent, jnp.zeros_like(cotangent))
    second_adj = (masked.astype(wide) * x0.astype(wide)).astype(low)
    bias_two = jnp.sum(second_adj.astype(wide), axis=0, keepdims=True)

    first_part = dot(x0, full_v).astype(low)
    whole_su = joined(own_su, 0, 1).reshape(width, rank)
    back_two_part = dot(second_adj, whole_su).astype(low)
    both = jnp.concatenate([first_part, back_two_part], 0)
    near, ring = near_groups(), ring_groups()
    other_u, shared_v, both = lax.optimization_barrier((other_u, shared_v, both))
    maps = joined(shared_v, 2, 0)
    part = summed(both, "feat", near)
    part, maps = lax.optimization_barrier((part, maps))
    maps = joined(joined(maps, 3, 0), 1, 2)
    part = summed(part, "feat", ring)
    part, maps = lax.optimization_barrier((part, maps))
    whole_sv = joined(maps, 0, 3).reshape(width, rank)
    part = gathered(part, "feat", ring)
    part, whole_sv, masked = lax.optimization_barrier((part, whole_sv, masked))
    sums = gathered(part, "feat", near)

    both, layer_one, first_adj, kept, bias_one = middle(sums, x0, masked, expert_u, other_u, whole_sv, bias)
    keep_eu, keep_sv, give = early_terms(core, first_adj, layer_one, sums, bias_one, bias_two, lines)
    part = summed(both, "feat", near)
    part, give = lax.optimization_barrier((part, give))
    part = summed(part, "feat", ring)
    part, give = lax.optimization_barrier((gathered(part, "feat", ring), give))
    peer = core_swap(give)
    sums = gathered(part, "feat", near)

    keep_su, give_su = late_terms(core, second_adj, sums, lines)
    sent = finished(keep_su, core_swap(give_su), keep_sv, peer, bias_one, bias_two)
    sent, sums = lax.optimization_barrier((sent, sums))
    taken = exchange(sent.reshape(-1, rank), "dom", chip_groups()).reshape(sent.shape)
    peer_eu = peer[:, :CHUNK, :half_rank].reshape(width, half_rank)
    grad_eu = (keep_eu + peer_eu.astype(wide)).astype(low)
    second_rank, back_one = sums[:rows], sums[rows:]
    partial_ev = transposed_dot(x0, back_one)
    peer_ev = core_swap(partial_ev[:, half_rank:].astype(low))
    grad_ev = (partial_ev[:, :half_rank] + peer_ev.astype(wide)).astype(low)
    second_gate = cross_dot(second_rank, whole_su) + bias[1][None, :]
    grad_inputs = (masked.astype(wide) * second_gate + kept + cross_dot(back_one, full_v)).astype(low)
    grad_su, grad_sv, grad_bias = last_sum(taken, lines, width)
    return (grad_inputs, grad_eu, grad_ev, grad_su, grad_sv, grad_bias)


def solution(mesh):
    placed = (
        P("dom", "feat"),
        P("dom", "feat"),
        P("dom"),
        P("feat", "dom"),
        P("feat", "dom"),
        P(("feat", "dom"), None),
        P(("feat", "dom"), None),
        P(None, "feat"),
    )
    return jax.shard_map(
        local,
        mesh=mesh,
        in_specs=placed,
        out_specs=(
            P("dom", "feat"),
            P("feat", "dom"),
            P("feat", "dom"),
            P(("feat", "dom"), None),
            P(("feat", "dom"), None),
            P(None, "feat"),
        ),
        check_vma=False,
    )
```

```python
import functools

import jax
import jax.numpy as jnp
from jax import lax
from jax.experimental import pallas as pl
from jax.experimental.pallas import tpu as pltpu
from jax.sharding import PartitionSpec as P

FAR = 2
CHUNK = 256
SPARE = 16
PARAMS = pltpu.CompilerParams(vmem_limit_bytes=32 * 1024 * 1024)


def core_swap(value):
    pairs = [(source, source ^ 1) for source in range(lax.axis_size("dom"))]
    return lax.ppermute(value, "dom", pairs)


def near_groups():
    half = lax.axis_size("feat") // FAR
    return [[far * half + 2 * pair + bit for far in range(FAR) for bit in range(2)] for pair in range(half // 2)]


def ring_groups():
    half = lax.axis_size("feat") // FAR
    return [[far * half + 2 * step + bit for step in range(half // 2)] for far in range(FAR) for bit in range(2)]


def chip_groups():
    return [list(range(core, lax.axis_size("dom"), 2)) for core in range(2)]


def exchange(value, axis, groups):
    return lax.all_to_all(value, axis, 0, 0, axis_index_groups=groups, tiled=True)


def gathered(value, axis, groups):
    members = len(groups[0])
    repeated = jnp.broadcast_to(value[None], (members, *value.shape))
    return exchange(repeated.reshape(members * value.shape[0], value.shape[1]), axis, groups)


def summed(value, axis, groups):
    pieces = exchange(value, axis, groups).reshape(len(groups[0]), -1, value.shape[1])
    return jnp.sum(pieces.astype(jnp.float32), axis=0).astype(jnp.bfloat16)


def dot(left_side, right_side):
    return jnp.dot(left_side, right_side, preferred_element_type=jnp.float32)


def transposed_dot(left_side, right_side):
    return lax.dot_general(
        left_side, right_side, (((0,), (0,)), ((), ())), preferred_element_type=jnp.float32
    )


def cross_dot(left_side, right_side):
    return lax.dot_general(
        left_side, right_side, (((1,), (1,)), ((), ())), preferred_element_type=jnp.float32
    )


def in_hbm(value):
    return pltpu.with_memory_space_constraint(value, pltpu.HBM)


def middle_kernel(
    place, sums, x0, masked, own_u, other_u, own_v, other_v, bias, both, layer_one, first_adj, kept, bias_sum, total, map_v
):
    low, wide = jnp.bfloat16, jnp.float32
    rows, half_rank = x0.shape[0], own_u.shape[1]
    chips, lines, _ = own_v.shape
    step = pl.program_id(0)

    def fill(pair):
        for chip in range(chips):
            for i, part in enumerate(pair):
                top = (2 * chip + i) * lines
                map_v[top : top + lines, :] = part[chip]

    @pl.when(place[0] == 0)
    def _():
        fill((own_v, other_v))

    @pl.when(place[0] != 0)
    def _():
        fill((other_v, own_v))

    @pl.when(step == 0)
    def _():
        total[...] = jnp.zeros_like(total)

    inputs = x0[...].astype(wide)
    first_gate = (
        cross_dot(sums[:rows, :half_rank], own_u[...])
        + cross_dot(sums[:rows, half_rank:], other_u[...])
        + bias[:1, :]
    )
    layer = (inputs * first_gate + inputs).astype(low)
    layer_grad = masked[...].astype(wide) + cross_dot(sums[rows:, :], map_v[...])
    adj = (layer_grad * inputs).astype(low)
    layer_one[...] = layer
    first_adj[...] = adj
    kept[...] = layer_grad * (first_gate + 1.0)
    bias_sum[...] = jnp.sum(adj.astype(wide), axis=0, keepdims=True)
    total[:rows, :] += dot(layer, map_v[...])
    total[rows:, :half_rank] += dot(adj, own_u[...])
    total[rows:, half_rank:] += dot(adj, other_u[...])

    @pl.when(step == pl.num_programs(0) - 1)
    def _():
        both[...] = total[...].astype(low)


def middle(core, sums, x0, masked, own_u, other_u, own_maps, other_maps, bias):
    low, wide = jnp.bfloat16, jnp.float32
    rows, width = x0.shape
    rank = sums.shape[1]
    lines = own_maps.shape[1] // 2
    across = pl.BlockSpec((rows, CHUNK), lambda i, place: (0, i))
    half = pl.BlockSpec((CHUNK, rank // 2), lambda i, place: (i, 0))
    fixed = pl.BlockSpec((2 * rows, rank), lambda i, place: (0, 0))
    map_rows = pl.BlockSpec((CHUNK // (2 * lines), lines, rank), lambda i, place: (i, 1, 0))
    return pl.pallas_call(
        middle_kernel,
        grid_spec=pltpu.PrefetchScalarGridSpec(
            num_scalar_prefetch=1,
            grid=(width // CHUNK,),
            in_specs=[
                fixed,
                across,
                across,
                half,
                half,
                map_rows,
                map_rows,
                pl.BlockSpec((2, CHUNK), lambda i, place: (0, i)),
            ],
            out_specs=[fixed, across, across, across, pl.BlockSpec((1, CHUNK), lambda i, place: (0, i))],
            scratch_shapes=[pltpu.VMEM((2 * rows, rank), wide), pltpu.VMEM((CHUNK, rank), low)],
        ),
        out_shape=[
            pltpu.HBM((2 * rows, rank), low),
            pltpu.HBM((rows, width), low),
            pltpu.HBM((rows, width), low),
            pltpu.HBM((rows, width), wide),
            jax.ShapeDtypeStruct((1, width), wide),
        ],
        compiler_params=PARAMS,
    )(core[None], sums, *map(in_hbm, (x0, masked, own_u, other_u, own_maps, other_maps)), bias)


def spread_kernel(map_u, map_v, out):
    lines = map_u.shape[0]
    for chip in range(out.shape[0]):
        out[chip, :lines, :] = map_u[...]
        out[chip, lines:, :] = map_v[...]


def spread(map_u, map_v, chips):
    lines, rank = map_u.shape
    rows = pl.BlockSpec((lines, rank), lambda i: (0, 0))
    return pl.pallas_call(
        spread_kernel,
        grid=(2,),
        in_specs=[rows, rows],
        out_specs=pl.BlockSpec((chips // 2, 2 * lines, rank), lambda i: (i, 0, 0)),
        out_shape=jax.ShapeDtypeStruct((chips, 2 * lines, rank), map_u.dtype),
        compiler_params=PARAMS,
    )(map_u, map_v)


def halves_of(term, core, pair, lines):
    first = term[2 * pair * lines : (2 * pair + 1) * lines]
    second = term[(2 * pair + 1) * lines : (2 * pair + 2) * lines]
    return jnp.where(core == 0, first, second), jnp.where(core == 0, second, first)


def in_two(line):
    high = line.astype(jnp.bfloat16).astype(jnp.float32)
    return high, (line - high).astype(jnp.bfloat16).astype(jnp.float32)


def early_kernel(place, first_adj, layer_one, sums, bias_one, bias_two, keep_u, keep_v, give):
    low = give.dtype
    rows, half_rank = first_adj.shape[0], keep_u.shape[1]
    pairs, lines, _ = keep_v.shape
    keep_u[...] = transposed_dot(first_adj[...], sums[:rows, :half_rank])
    give[0, :CHUNK, :half_rank] = transposed_dot(first_adj[...], sums[:rows, half_rank:]).astype(low)
    term = transposed_dot(layer_one[...], sums[rows:, :])
    for pair in range(pairs):
        keep_v[pair], away = halves_of(term, place[0], pair, lines)
        top = 2 * pair * lines
        give[0, top : top + lines, half_rank:] = away[:, :half_rank].astype(low)
        give[0, top + lines : top + 2 * lines, half_rank:] = away[:, half_rank:].astype(low)
    one = jnp.concatenate(in_two(bias_one[...]), 1)
    two = jnp.concatenate(in_two(bias_two[...]), 1)
    row = lax.broadcasted_iota(jnp.int32, (SPARE, one.shape[1]), 0)
    give[0, CHUNK:, :] = jnp.where(row == 0, one, jnp.where(row == 1, two, 0.0)).astype(low)


def early_terms(core, first_adj, layer_one, sums, bias_one, bias_two, lines):
    low, wide = jnp.bfloat16, jnp.float32
    rows, width = first_adj.shape
    rank = sums.shape[1]
    pairs = CHUNK // (2 * lines)
    chunks = width // CHUNK
    across = pl.BlockSpec((rows, CHUNK), lambda i, place: (0, i))
    line = pl.BlockSpec((1, CHUNK), lambda i, place: (0, i))
    return pl.pallas_call(
        early_kernel,
        grid_spec=pltpu.PrefetchScalarGridSpec(
            num_scalar_prefetch=1,
            grid=(chunks,),
            in_specs=[across, across, pl.BlockSpec(sums.shape, lambda i, place: (0, 0)), line, line],
            out_specs=[
                pl.BlockSpec((CHUNK, rank // 2), lambda i, place: (i, 0)),
                pl.BlockSpec((pairs, lines, rank), lambda i, place: (i, 0, 0)),
                pl.BlockSpec((1, CHUNK + SPARE, rank), lambda i, place: (i, 0, 0)),
            ],
        ),
        out_shape=[
            pltpu.HBM((width, rank // 2), wide),
            pltpu.HBM((width // (2 * lines), lines, rank), wide),
            pltpu.HBM((chunks, CHUNK + SPARE, rank), low),
        ],
        compiler_params=PARAMS,
    )(core[None], in_hbm(first_adj), in_hbm(layer_one), sums, bias_one, bias_two)


def finish_kernel(keep_u, give_u, keep_v, peer, bias_one, bias_two, sent):
    low, wide = sent.dtype, jnp.float32
    chips, lines, rank = keep_v.shape
    half_rank = rank // 2
    chunks = peer.shape[0]
    pairs = chips // chunks
    tail = jnp.zeros((SPARE, rank), wide)
    row = lax.broadcasted_iota(jnp.int32, tail.shape, 0)
    for i in range(chunks):
        for pair in range(pairs):
            top = 2 * pair * lines
            left = peer[i, top : top + lines, half_rank:].astype(wide)
            right = peer[i, top + lines : top + 2 * lines, half_rank:].astype(wide)
            chip = i * pairs + pair
            sent[chip, :lines, :] = (keep_u[chip] + give_u[chip].astype(wide)).astype(low)
            sent[chip, lines : 2 * lines, :half_rank] = (keep_v[chip, :, :half_rank] + left).astype(low)
            sent[chip, lines : 2 * lines, half_rank:] = (keep_v[chip, :, half_rank:] + right).astype(low)
        theirs = peer[i, CHUNK:, :].astype(wide)
        theirs = theirs[:, :half_rank] + theirs[:, half_rank:]
        spot = slice(i * CHUNK, (i + 1) * CHUNK)
        for t, bias in enumerate((bias_one, bias_two)):
            high, rest = in_two(bias[:, spot])
            line = jnp.concatenate(in_two((high + rest) + theirs[t : t + 1]), 1)
            tail = jnp.where(row == 2 * i + t, line, tail)
    for chip in range(chips):
        sent[chip, 2 * lines :, :] = tail.astype(low)


def finished(keep_u, peer_u, keep_v, peer, bias_one, bias_two):
    chips, lines, rank = keep_v.shape
    return pl.pallas_call(
        finish_kernel,
        out_shape=jax.ShapeDtypeStruct((chips, 2 * lines + SPARE, rank), jnp.bfloat16),
        compiler_params=PARAMS,
    )(keep_u, peer_u, keep_v, peer, bias_one, bias_two)


def late_kernel(place, second_adj, sums, keep, give):
    rows = second_adj.shape[0]
    pairs, lines, _ = keep.shape
    term = transposed_dot(second_adj[...], sums[:rows, :])
    for pair in range(pairs):
        keep[pair], away = halves_of(term, place[0], pair, lines)
        give[pair] = away.astype(give.dtype)


def late_terms(core, second_adj, sums, lines):
    rows, width = second_adj.shape
    rank = sums.shape[1]
    shared = pl.BlockSpec((CHUNK // (2 * lines), lines, rank), lambda i, place: (i, 0, 0))
    shape = (width // (2 * lines), lines, rank)
    return pl.pallas_call(
        late_kernel,
        grid_spec=pltpu.PrefetchScalarGridSpec(
            num_scalar_prefetch=1,
            grid=(width // CHUNK,),
            in_specs=[
                pl.BlockSpec((rows, CHUNK), lambda i, place: (0, i)),
                pl.BlockSpec(sums.shape, lambda i, place: (0, 0)),
            ],
            out_specs=[shared, shared],
        ),
        out_shape=[jax.ShapeDtypeStruct(shape, jnp.float32), jax.ShapeDtypeStruct(shape, jnp.bfloat16)],
        compiler_params=PARAMS,
    )(core[None], second_adj, sums)


def last_kernel(lines, taken, grad_su, grad_sv, grad_bias):
    low, wide = jnp.bfloat16, jnp.float32
    total = jnp.sum(taken[...].astype(wide), axis=0)
    grad_su[...] = total[:lines].astype(low)
    grad_sv[...] = total[lines : 2 * lines].astype(low)
    sums = total[2 * lines :]
    sums = sums[:, : sums.shape[1] // 2] + sums[:, sums.shape[1] // 2 :]
    for i in range(grad_bias.shape[1] // CHUNK):
        grad_bias[:, i * CHUNK : (i + 1) * CHUNK] = sums[2 * i : 2 * i + 2]


def last_sum(taken, lines, width):
    rank = taken.shape[2]
    return pl.pallas_call(
        functools.partial(last_kernel, lines),
        out_shape=[
            jax.ShapeDtypeStruct((lines, rank), jnp.bfloat16),
            jax.ShapeDtypeStruct((lines, rank), jnp.bfloat16),
            jax.ShapeDtypeStruct((2, width), jnp.float32),
        ],
        compiler_params=PARAMS,
    )(taken)


def local(x0, cotangent, domain_ids, expert_u, expert_v, shared_u, shared_v, bias):
    low = jnp.bfloat16
    wide = jnp.float32
    rows, width = x0.shape
    half_rank = expert_u.shape[1]
    rank = 2 * half_rank
    chips = lax.axis_size("dom") // 2
    lines = shared_u.shape[0]
    domain = lax.axis_index("dom") // 2
    core = lax.axis_index("dom") % 2

    maps = spread(shared_u, shared_v, chips)
    maps, expert_u, expert_v = lax.optimization_barrier((maps, expert_u, expert_v))
    own_maps = exchange(maps.reshape(-1, rank), "dom", chip_groups()).reshape(maps.shape)
    other_maps = core_swap(own_maps)
    other_v = core_swap(expert_v)
    other_u = core_swap(expert_u)
    full_v = jnp.concatenate([expert_v, other_v], 1)

    masked = jnp.where((domain_ids == domain)[:, None], cotangent, jnp.zeros_like(cotangent))
    second_adj = (masked.astype(wide) * x0.astype(wide)).astype(low)
    bias_two = jnp.sum(second_adj.astype(wide), axis=0, keepdims=True)

    first_part = dot(x0, full_v).astype(low)
    own_su, other_su = own_maps[:, :lines], other_maps[:, :lines]
    pair = [jnp.where(core == 0, own_su, other_su), jnp.where(core == 0, other_su, own_su)]
    whole_su = jnp.stack(pair, 1).reshape(width, rank)
    back_two_part = dot(second_adj, whole_su).astype(low)
    both = jnp.concatenate([first_part, back_two_part], 0)
    near, ring = near_groups(), ring_groups()
    other_u, both = lax.optimization_barrier((other_u, both))
    part = summed(summed(both, "feat", near), "feat", ring)
    sums = gathered(gathered(part, "feat", ring), "feat", near)

    both, layer_one, first_adj, kept, bias_one = middle(
        core, sums, x0, masked, expert_u, other_u, own_maps, other_maps, bias
    )
    keep_eu, keep_sv, give = early_terms(core, first_adj, layer_one, sums, bias_one, bias_two, lines)
    part = summed(both, "feat", near)
    part, give = lax.optimization_barrier((part, give))
    part = summed(part, "feat", ring)
    part, give = lax.optimization_barrier((gathered(part, "feat", ring), give))
    peer = core_swap(give)
    sums = gathered(part, "feat", near)

    keep_su, give_su = late_terms(core, second_adj, sums, lines)
    sent = finished(keep_su, core_swap(give_su), keep_sv, peer, bias_one, bias_two)
    sent, sums = lax.optimization_barrier((sent, sums))
    taken = exchange(sent.reshape(-1, rank), "dom", chip_groups()).reshape(sent.shape)
    peer_eu = peer[:, :CHUNK, :half_rank].reshape(width, half_rank)
    grad_eu = (keep_eu + peer_eu.astype(wide)).astype(low)
    second_rank, back_one = sums[:rows], sums[rows:]
    partial_ev = transposed_dot(x0, back_one)
    peer_ev = core_swap(partial_ev[:, half_rank:].astype(low))
    grad_ev = (partial_ev[:, :half_rank] + peer_ev.astype(wide)).astype(low)
    second_gate = cross_dot(second_rank, whole_su) + bias[1][None, :]
    grad_inputs = (masked.astype(wide) * second_gate + kept + cross_dot(back_one, full_v)).astype(low)
    grad_su, grad_sv, grad_bias = last_sum(taken, lines, width)
    return (grad_inputs, grad_eu, grad_ev, grad_su, grad_sv, grad_bias)


def solution(mesh):
    placed = (
        P("dom", "feat"),
        P("dom", "feat"),
        P("dom"),
        P("feat", "dom"),
        P("feat", "dom"),
        P(("feat", "dom"), None),
        P(("feat", "dom"), None),
        P(None, "feat"),
    )
    return jax.shard_map(
        local,
        mesh=mesh,
        in_specs=placed,
        out_specs=(
            P("dom", "feat"),
            P("feat", "dom"),
            P("feat", "dom"),
            P(("feat", "dom"), None),
            P(("feat", "dom"), None),
            P(None, "feat"),
        ),
        check_vma=False,
    )
```

```python
import functools

import jax
import jax.numpy as jnp
from jax import lax
from jax.experimental import pallas as pl
from jax.experimental.pallas import tpu as pltpu
from jax.sharding import PartitionSpec as P

FAR = 2
CHUNK = 256
SPARE = 16
PARAMS = pltpu.CompilerParams(vmem_limit_bytes=32 * 1024 * 1024)


def core_swap(value):
    pairs = [(source, source ^ 1) for source in range(lax.axis_size("dom"))]
    return lax.ppermute(value, "dom", pairs)


def near_groups():
    half = lax.axis_size("feat") // FAR
    return [[far * half + 2 * pair + bit for far in range(FAR) for bit in range(2)] for pair in range(half // 2)]


def ring_groups():
    half = lax.axis_size("feat") // FAR
    return [[far * half + 2 * step + bit for step in range(half // 2)] for far in range(FAR) for bit in range(2)]


def chip_groups():
    return [list(range(core, lax.axis_size("dom"), 2)) for core in range(2)]


def exchange(value, axis, groups):
    return lax.all_to_all(value, axis, 0, 0, axis_index_groups=groups, tiled=True)


def gathered(value, axis, groups):
    members = len(groups[0])
    repeated = jnp.broadcast_to(value[None], (members, *value.shape))
    return exchange(repeated.reshape(members * value.shape[0], value.shape[1]), axis, groups)


def summed(value, axis, groups):
    pieces = exchange(value, axis, groups).reshape(len(groups[0]), -1, value.shape[1])
    return jnp.sum(pieces.astype(jnp.float32), axis=0).astype(jnp.bfloat16)


def dot(left_side, right_side):
    return jnp.dot(left_side, right_side, preferred_element_type=jnp.float32)


def transposed_dot(left_side, right_side):
    return lax.dot_general(
        left_side, right_side, (((0,), (0,)), ((), ())), preferred_element_type=jnp.float32
    )


def cross_dot(left_side, right_side):
    return lax.dot_general(
        left_side, right_side, (((1,), (1,)), ((), ())), preferred_element_type=jnp.float32
    )


def in_hbm(value):
    return pltpu.with_memory_space_constraint(value, pltpu.HBM)


def middle_kernel(
    place, sums, x0, masked, own_u, other_u, own_v, other_v, bias, both, layer_one, first_adj, kept, bias_sum, total, map_v
):
    low, wide = jnp.bfloat16, jnp.float32
    rows, half_rank = x0.shape[0], own_u.shape[1]
    chips, lines, _ = own_v.shape
    step = pl.program_id(0)

    def fill(pair):
        for chip in range(chips):
            for i, part in enumerate(pair):
                top = (2 * chip + i) * lines
                map_v[top : top + lines, :] = part[chip]

    @pl.when(place[0] == 0)
    def _():
        fill((own_v, other_v))

    @pl.when(place[0] != 0)
    def _():
        fill((other_v, own_v))

    @pl.when(step == 0)
    def _():
        total[...] = jnp.zeros_like(total)

    inputs = x0[...].astype(wide)
    first_gate = (
        cross_dot(sums[:rows, :half_rank], own_u[...])
        + cross_dot(sums[:rows, half_rank:], other_u[...])
        + bias[:1, :]
    )
    layer = (inputs * first_gate + inputs).astype(low)
    layer_grad = masked[...].astype(wide) + cross_dot(sums[rows:, :], map_v[...])
    adj = (layer_grad * inputs).astype(low)
    layer_one[...] = layer
    first_adj[...] = adj
    kept[...] = layer_grad * (first_gate + 1.0)
    bias_sum[...] = jnp.sum(adj.astype(wide), axis=0, keepdims=True)
    total[:rows, :] += dot(layer, map_v[...])
    total[rows:, :half_rank] += dot(adj, own_u[...])
    total[rows:, half_rank:] += dot(adj, other_u[...])

    @pl.when(step == pl.num_programs(0) - 1)
    def _():
        both[...] = total[...].astype(low)


def middle(core, sums, x0, masked, own_u, other_u, own_maps, other_maps, bias):
    low, wide = jnp.bfloat16, jnp.float32
    rows, width = x0.shape
    rank = sums.shape[1]
    lines = own_maps.shape[1] // 2
    across = pl.BlockSpec((rows, CHUNK), lambda i, place: (0, i))
    half = pl.BlockSpec((CHUNK, rank // 2), lambda i, place: (i, 0))
    fixed = pl.BlockSpec((2 * rows, rank), lambda i, place: (0, 0))
    map_rows = pl.BlockSpec((CHUNK // (2 * lines), lines, rank), lambda i, place: (i, 1, 0))
    return pl.pallas_call(
        middle_kernel,
        grid_spec=pltpu.PrefetchScalarGridSpec(
            num_scalar_prefetch=1,
            grid=(width // CHUNK,),
            in_specs=[
                fixed,
                across,
                across,
                half,
                half,
                map_rows,
                map_rows,
                pl.BlockSpec((2, CHUNK), lambda i, place: (0, i)),
            ],
            out_specs=[fixed, across, across, across, pl.BlockSpec((1, CHUNK), lambda i, place: (0, i))],
            scratch_shapes=[pltpu.VMEM((2 * rows, rank), wide), pltpu.VMEM((CHUNK, rank), low)],
        ),
        out_shape=[
            pltpu.HBM((2 * rows, rank), low),
            pltpu.HBM((rows, width), low),
            pltpu.HBM((rows, width), low),
            pltpu.HBM((rows, width), wide),
            jax.ShapeDtypeStruct((1, width), wide),
        ],
        compiler_params=PARAMS,
    )(core[None], sums, *map(in_hbm, (x0, masked, own_u, other_u, own_maps, other_maps)), bias)


def spread_kernel(map_u, map_v, out):
    lines = map_u.shape[0]
    for chip in range(out.shape[0]):
        out[chip, :lines, :] = map_u[...]
        out[chip, lines:, :] = map_v[...]


def spread(map_u, map_v, chips):
    lines, rank = map_u.shape
    rows = pl.BlockSpec((lines, rank), lambda i: (0, 0))
    return pl.pallas_call(
        spread_kernel,
        grid=(2,),
        in_specs=[rows, rows],
        out_specs=pl.BlockSpec((chips // 2, 2 * lines, rank), lambda i: (i, 0, 0)),
        out_shape=jax.ShapeDtypeStruct((chips, 2 * lines, rank), map_u.dtype),
        compiler_params=PARAMS,
    )(in_hbm(map_u), in_hbm(map_v))


def halves_of(term, core, pair, lines):
    first = term[2 * pair * lines : (2 * pair + 1) * lines]
    second = term[(2 * pair + 1) * lines : (2 * pair + 2) * lines]
    return jnp.where(core == 0, first, second), jnp.where(core == 0, second, first)


def in_two(line):
    high = line.astype(jnp.bfloat16).astype(jnp.float32)
    return high, (line - high).astype(jnp.bfloat16).astype(jnp.float32)


def early_kernel(place, first_adj, layer_one, sums, bias_one, bias_two, keep_u, keep_v, give):
    low = give.dtype
    rows, half_rank = first_adj.shape[0], keep_u.shape[1]
    pairs, lines, _ = keep_v.shape
    keep_u[...] = transposed_dot(first_adj[...], sums[:rows, :half_rank])
    give[0, :CHUNK, :half_rank] = transposed_dot(first_adj[...], sums[:rows, half_rank:]).astype(low)
    term = transposed_dot(layer_one[...], sums[rows:, :])
    for pair in range(pairs):
        keep_v[pair], away = halves_of(term, place[0], pair, lines)
        top = 2 * pair * lines
        give[0, top : top + lines, half_rank:] = away[:, :half_rank].astype(low)
        give[0, top + lines : top + 2 * lines, half_rank:] = away[:, half_rank:].astype(low)
    one = jnp.concatenate(in_two(bias_one[...]), 1)
    two = jnp.concatenate(in_two(bias_two[...]), 1)
    row = lax.broadcasted_iota(jnp.int32, (SPARE, one.shape[1]), 0)
    give[0, CHUNK:, :] = jnp.where(row == 0, one, jnp.where(row == 1, two, 0.0)).astype(low)


def early_terms(core, first_adj, layer_one, sums, bias_one, bias_two, lines):
    low, wide = jnp.bfloat16, jnp.float32
    rows, width = first_adj.shape
    rank = sums.shape[1]
    pairs = CHUNK // (2 * lines)
    chunks = width // CHUNK
    across = pl.BlockSpec((rows, CHUNK), lambda i, place: (0, i))
    line = pl.BlockSpec((1, CHUNK), lambda i, place: (0, i))
    return pl.pallas_call(
        early_kernel,
        grid_spec=pltpu.PrefetchScalarGridSpec(
            num_scalar_prefetch=1,
            grid=(chunks,),
            in_specs=[across, across, pl.BlockSpec(sums.shape, lambda i, place: (0, 0)), line, line],
            out_specs=[
                pl.BlockSpec((CHUNK, rank // 2), lambda i, place: (i, 0)),
                pl.BlockSpec((pairs, lines, rank), lambda i, place: (i, 0, 0)),
                pl.BlockSpec((1, CHUNK + SPARE, rank), lambda i, place: (i, 0, 0)),
            ],
        ),
        out_shape=[
            pltpu.HBM((width, rank // 2), wide),
            pltpu.HBM((width // (2 * lines), lines, rank), wide),
            pltpu.HBM((chunks, CHUNK + SPARE, rank), low),
        ],
        compiler_params=PARAMS,
    )(core[None], in_hbm(first_adj), in_hbm(layer_one), sums, bias_one, bias_two)


def finish_kernel(keep_u, give_u, keep_v, peer, bias_one, bias_two, sent):
    low, wide = sent.dtype, jnp.float32
    chips, lines, rank = keep_v.shape
    half_rank = rank // 2
    chunks = peer.shape[0]
    pairs = chips // chunks
    tail = jnp.zeros((SPARE, rank), wide)
    row = lax.broadcasted_iota(jnp.int32, tail.shape, 0)
    for i in range(chunks):
        for pair in range(pairs):
            top = 2 * pair * lines
            left = peer[i, top : top + lines, half_rank:].astype(wide)
            right = peer[i, top + lines : top + 2 * lines, half_rank:].astype(wide)
            chip = i * pairs + pair
            sent[chip, :lines, :] = (keep_u[chip] + give_u[chip].astype(wide)).astype(low)
            sent[chip, lines : 2 * lines, :half_rank] = (keep_v[chip, :, :half_rank] + left).astype(low)
            sent[chip, lines : 2 * lines, half_rank:] = (keep_v[chip, :, half_rank:] + right).astype(low)
        theirs = peer[i, CHUNK:, :].astype(wide)
        theirs = theirs[:, :half_rank] + theirs[:, half_rank:]
        spot = slice(i * CHUNK, (i + 1) * CHUNK)
        for t, bias in enumerate((bias_one, bias_two)):
            high, rest = in_two(bias[:, spot])
            line = jnp.concatenate(in_two((high + rest) + theirs[t : t + 1]), 1)
            tail = jnp.where(row == 2 * i + t, line, tail)
    for chip in range(chips):
        sent[chip, 2 * lines :, :] = tail.astype(low)


def finished(keep_u, peer_u, keep_v, peer, bias_one, bias_two):
    chips, lines, rank = keep_v.shape
    return pl.pallas_call(
        finish_kernel,
        out_shape=jax.ShapeDtypeStruct((chips, 2 * lines + SPARE, rank), jnp.bfloat16),
        compiler_params=PARAMS,
    )(keep_u, peer_u, keep_v, peer, bias_one, bias_two)


def late_kernel(place, second_adj, sums, keep, give):
    rows = second_adj.shape[0]
    pairs, lines, _ = keep.shape
    term = transposed_dot(second_adj[...], sums[:rows, :])
    for pair in range(pairs):
        keep[pair], away = halves_of(term, place[0], pair, lines)
        give[pair] = away.astype(give.dtype)


def late_terms(core, second_adj, sums, lines):
    rows, width = second_adj.shape
    rank = sums.shape[1]
    shared = pl.BlockSpec((CHUNK // (2 * lines), lines, rank), lambda i, place: (i, 0, 0))
    shape = (width // (2 * lines), lines, rank)
    return pl.pallas_call(
        late_kernel,
        grid_spec=pltpu.PrefetchScalarGridSpec(
            num_scalar_prefetch=1,
            grid=(width // CHUNK,),
            in_specs=[
                pl.BlockSpec((rows, CHUNK), lambda i, place: (0, i)),
                pl.BlockSpec(sums.shape, lambda i, place: (0, 0)),
            ],
            out_specs=[shared, shared],
        ),
        out_shape=[jax.ShapeDtypeStruct(shape, jnp.float32), jax.ShapeDtypeStruct(shape, jnp.bfloat16)],
        compiler_params=PARAMS,
    )(core[None], second_adj, sums)


def last_kernel(lines, taken, grad_su, grad_sv, grad_bias):
    low, wide = jnp.bfloat16, jnp.float32
    total = jnp.sum(taken[...].astype(wide), axis=0)
    grad_su[...] = total[:lines].astype(low)
    grad_sv[...] = total[lines : 2 * lines].astype(low)
    sums = total[2 * lines :]
    sums = sums[:, : sums.shape[1] // 2] + sums[:, sums.shape[1] // 2 :]
    for i in range(grad_bias.shape[1] // CHUNK):
        grad_bias[:, i * CHUNK : (i + 1) * CHUNK] = sums[2 * i : 2 * i + 2]


def last_sum(taken, lines, width):
    rank = taken.shape[2]
    return pl.pallas_call(
        functools.partial(last_kernel, lines),
        out_shape=[
            jax.ShapeDtypeStruct((lines, rank), jnp.bfloat16),
            jax.ShapeDtypeStruct((lines, rank), jnp.bfloat16),
            jax.ShapeDtypeStruct((2, width), jnp.float32),
        ],
        compiler_params=PARAMS,
    )(taken)


def local(x0, cotangent, domain_ids, expert_u, expert_v, shared_u, shared_v, bias):
    low = jnp.bfloat16
    wide = jnp.float32
    rows, width = x0.shape
    half_rank = expert_u.shape[1]
    rank = 2 * half_rank
    chips = lax.axis_size("dom") // 2
    lines = shared_u.shape[0]
    domain = lax.axis_index("dom") // 2
    core = lax.axis_index("dom") % 2

    maps = spread(shared_u, shared_v, chips)
    maps, expert_u, expert_v = lax.optimization_barrier((maps, expert_u, expert_v))
    own_maps = exchange(maps.reshape(-1, rank), "dom", chip_groups()).reshape(maps.shape)
    other_v = core_swap(expert_v)
    other_u = core_swap(expert_u)
    full_v = jnp.concatenate([expert_v, other_v], 1)

    masked = jnp.where((domain_ids == domain)[:, None], cotangent, jnp.zeros_like(cotangent))
    second_adj = (masked.astype(wide) * x0.astype(wide)).astype(low)
    bias_two = jnp.sum(second_adj.astype(wide), axis=0, keepdims=True)

    first_part = dot(x0, full_v).astype(low)
    own_maps, first_part, second_adj, bias_two = lax.optimization_barrier((own_maps, first_part, second_adj, bias_two))
    other_maps = core_swap(own_maps)
    own_su, other_su = own_maps[:, :lines], other_maps[:, :lines]
    pair = [jnp.where(core == 0, own_su, other_su), jnp.where(core == 0, other_su, own_su)]
    whole_su = jnp.stack(pair, 1).reshape(width, rank)
    back_two_part = dot(second_adj, whole_su).astype(low)
    both = jnp.concatenate([first_part, back_two_part], 0)
    near, ring = near_groups(), ring_groups()
    other_u, both = lax.optimization_barrier((other_u, both))
    part = summed(summed(both, "feat", near), "feat", ring)
    sums = gathered(gathered(part, "feat", ring), "feat", near)

    both, layer_one, first_adj, kept, bias_one = middle(
        core, sums, x0, masked, expert_u, other_u, own_maps, other_maps, bias
    )
    keep_eu, keep_sv, give = early_terms(core, first_adj, layer_one, sums, bias_one, bias_two, lines)
    part = summed(both, "feat", near)
    part, give = lax.optimization_barrier((part, give))
    part = summed(part, "feat", ring)
    part, give = lax.optimization_barrier((gathered(part, "feat", ring), give))
    peer = core_swap(give)
    sums = gathered(part, "feat", near)

    keep_su, give_su = late_terms(core, second_adj, sums, lines)
    sent = finished(keep_su, core_swap(give_su), keep_sv, peer, bias_one, bias_two)
    sent, sums = lax.optimization_barrier((sent, sums))
    taken = exchange(sent.reshape(-1, rank), "dom", chip_groups()).reshape(sent.shape)
    peer_eu = peer[:, :CHUNK, :half_rank].reshape(width, half_rank)
    grad_eu = (keep_eu + peer_eu.astype(wide)).astype(low)
    second_rank, back_one = sums[:rows], sums[rows:]
    partial_ev = transposed_dot(x0, back_one)
    peer_ev = core_swap(partial_ev[:, half_rank:].astype(low))
    grad_ev = (partial_ev[:, :half_rank] + peer_ev.astype(wide)).astype(low)
    second_gate = cross_dot(second_rank, whole_su) + bias[1][None, :]
    grad_inputs = (masked.astype(wide) * second_gate + kept + cross_dot(back_one, full_v)).astype(low)
    grad_su, grad_sv, grad_bias = last_sum(taken, lines, width)
    return (grad_inputs, grad_eu, grad_ev, grad_su, grad_sv, grad_bias)


def solution(mesh):
    placed = (
        P("dom", "feat"),
        P("dom", "feat"),
        P("dom"),
        P("feat", "dom"),
        P("feat", "dom"),
        P(("feat", "dom"), None),
        P(("feat", "dom"), None),
        P(None, "feat"),
    )
    return jax.shard_map(
        local,
        mesh=mesh,
        in_specs=placed,
        out_specs=(
            P("dom", "feat"),
            P("feat", "dom"),
            P("feat", "dom"),
            P(("feat", "dom"), None),
            P(("feat", "dom"), None),
            P(None, "feat"),
        ),
        check_vma=False,
    )
```

```python
import functools

import jax
import jax.numpy as jnp
from jax import lax
from jax.experimental import pallas as pl
from jax.experimental.pallas import tpu as pltpu
from jax.sharding import PartitionSpec as P

FAR = 2
CHUNK = 256
MIDDLE_CHUNK = 512
SPARE = 16
PARAMS = pltpu.CompilerParams(vmem_limit_bytes=32 * 1024 * 1024)


def core_swap(value):
    pairs = [(source, source ^ 1) for source in range(lax.axis_size("dom"))]
    return lax.ppermute(value, "dom", pairs)


def near_groups():
    half = lax.axis_size("feat") // FAR
    return [[far * half + 2 * pair + bit for far in range(FAR) for bit in range(2)] for pair in range(half // 2)]


def ring_groups():
    half = lax.axis_size("feat") // FAR
    return [[far * half + 2 * step + bit for step in range(half // 2)] for far in range(FAR) for bit in range(2)]


def chip_groups():
    return [list(range(core, lax.axis_size("dom"), 2)) for core in range(2)]


def exchange(value, axis, groups):
    return lax.all_to_all(value, axis, 0, 0, axis_index_groups=groups, tiled=True)


def gathered(value, axis, groups):
    members = len(groups[0])
    repeated = jnp.broadcast_to(value[None], (members, *value.shape))
    return exchange(repeated.reshape(members * value.shape[0], value.shape[1]), axis, groups)


def summed(value, axis, groups):
    pieces = exchange(value, axis, groups).reshape(len(groups[0]), -1, value.shape[1])
    return jnp.sum(pieces.astype(jnp.float32), axis=0).astype(jnp.bfloat16)


def dot(left_side, right_side):
    return jnp.dot(left_side, right_side, preferred_element_type=jnp.float32)


def transposed_dot(left_side, right_side):
    return lax.dot_general(
        left_side, right_side, (((0,), (0,)), ((), ())), preferred_element_type=jnp.float32
    )


def cross_dot(left_side, right_side):
    return lax.dot_general(
        left_side, right_side, (((1,), (1,)), ((), ())), preferred_element_type=jnp.float32
    )


def in_hbm(value):
    return pltpu.with_memory_space_constraint(value, pltpu.HBM)


def middle_kernel(
    place, sums, x0, masked, own_u, other_u, own_v, other_v, bias, both, layer_one, first_adj, kept, bias_sum, total, map_v
):
    low, wide = jnp.bfloat16, jnp.float32
    rows, half_rank = x0.shape[0], own_u.shape[1]
    chips, lines, _ = own_v.shape
    step = pl.program_id(0)

    def fill(pair):
        for chip in range(chips):
            for i, part in enumerate(pair):
                top = (2 * chip + i) * lines
                map_v[top : top + lines, :] = part[chip]

    @pl.when(place[0] == 0)
    def _():
        fill((own_v, other_v))

    @pl.when(place[0] != 0)
    def _():
        fill((other_v, own_v))

    inputs = x0[...].astype(wide)
    first_gate = (
        cross_dot(sums[:rows, :half_rank], own_u[...])
        + cross_dot(sums[:rows, half_rank:], other_u[...])
        + bias[:1, :]
    )
    layer = (inputs * first_gate + inputs).astype(low)
    layer_grad = masked[...].astype(wide) + cross_dot(sums[rows:, :], map_v[...])
    adj = (layer_grad * inputs).astype(low)
    layer_one[...] = layer
    first_adj[...] = adj
    kept[...] = layer_grad * (first_gate + 1.0)
    bias_sum[...] = jnp.sum(adj.astype(wide), axis=0, keepdims=True)
    parts = (
        (slice(0, rows), slice(None), dot(layer, map_v[...])),
        (slice(rows, None), slice(0, half_rank), dot(adj, own_u[...])),
        (slice(rows, None), slice(half_rank, None), dot(adj, other_u[...])),
    )
    last = pl.num_programs(0) - 1

    @pl.when(step == 0)
    def _():
        for across, along, part in parts:
            total[across, along] = part

    @pl.when(jnp.logical_and(step > 0, step < last))
    def _():
        for across, along, part in parts:
            total[across, along] += part

    @pl.when(step == last)
    def _():
        for across, along, part in parts:
            both[across, along] = (total[across, along] + part).astype(low)


def middle(core, sums, x0, masked, own_u, other_u, own_maps, other_maps, bias):
    low, wide = jnp.bfloat16, jnp.float32
    rows, width = x0.shape
    rank = sums.shape[1]
    lines = own_maps.shape[1] // 2
    across = pl.BlockSpec((rows, MIDDLE_CHUNK), lambda i, place: (0, i))
    half = pl.BlockSpec((MIDDLE_CHUNK, rank // 2), lambda i, place: (i, 0))
    fixed = pl.BlockSpec((2 * rows, rank), lambda i, place: (0, 0))
    map_rows = pl.BlockSpec((MIDDLE_CHUNK // (2 * lines), lines, rank), lambda i, place: (i, 1, 0))
    return pl.pallas_call(
        middle_kernel,
        grid_spec=pltpu.PrefetchScalarGridSpec(
            num_scalar_prefetch=1,
            grid=(width // MIDDLE_CHUNK,),
            in_specs=[
                fixed,
                across,
                across,
                half,
                half,
                map_rows,
                map_rows,
                pl.BlockSpec((2, MIDDLE_CHUNK), lambda i, place: (0, i)),
            ],
            out_specs=[fixed, across, across, across, pl.BlockSpec((1, MIDDLE_CHUNK), lambda i, place: (0, i))],
            scratch_shapes=[pltpu.VMEM((2 * rows, rank), wide), pltpu.VMEM((MIDDLE_CHUNK, rank), low)],
        ),
        out_shape=[
            pltpu.HBM((2 * rows, rank), low),
            pltpu.HBM((rows, width), low),
            pltpu.HBM((rows, width), low),
            pltpu.HBM((rows, width), wide),
            jax.ShapeDtypeStruct((1, width), wide),
        ],
        compiler_params=PARAMS,
    )(core[None], sums, *map(in_hbm, (x0, masked, own_u, other_u, own_maps, other_maps)), bias)


def spread_kernel(map_u, map_v, out):
    lines = map_u.shape[0]
    for chip in range(out.shape[0]):
        out[chip, :lines, :] = map_u[...]
        out[chip, lines:, :] = map_v[...]


def spread(map_u, map_v, chips):
    lines, rank = map_u.shape
    rows = pl.BlockSpec((lines, rank), lambda i: (0, 0))
    return pl.pallas_call(
        spread_kernel,
        grid=(2,),
        in_specs=[rows, rows],
        out_specs=pl.BlockSpec((chips // 2, 2 * lines, rank), lambda i: (i, 0, 0)),
        out_shape=jax.ShapeDtypeStruct((chips, 2 * lines, rank), map_u.dtype),
        compiler_params=PARAMS,
    )(in_hbm(map_u), in_hbm(map_v))


def halves_of(term, core, pair, lines):
    first = term[2 * pair * lines : (2 * pair + 1) * lines]
    second = term[(2 * pair + 1) * lines : (2 * pair + 2) * lines]
    return jnp.where(core == 0, first, second), jnp.where(core == 0, second, first)


def in_two(line):
    high = line.astype(jnp.bfloat16).astype(jnp.float32)
    return high, (line - high).astype(jnp.bfloat16).astype(jnp.float32)


def early_kernel(place, first_adj, layer_one, sums, bias_one, bias_two, keep_u, keep_v, give):
    low = give.dtype
    rows, half_rank = first_adj.shape[0], keep_u.shape[1]
    pairs, lines, _ = keep_v.shape
    keep_u[...] = transposed_dot(first_adj[...], sums[:rows, :half_rank])
    give[0, :CHUNK, :half_rank] = transposed_dot(first_adj[...], sums[:rows, half_rank:]).astype(low)
    term = transposed_dot(layer_one[...], sums[rows:, :])
    for pair in range(pairs):
        keep_v[pair], away = halves_of(term, place[0], pair, lines)
        top = 2 * pair * lines
        give[0, top : top + lines, half_rank:] = away[:, :half_rank].astype(low)
        give[0, top + lines : top + 2 * lines, half_rank:] = away[:, half_rank:].astype(low)
    one = jnp.concatenate(in_two(bias_one[...]), 1)
    two = jnp.concatenate(in_two(bias_two[...]), 1)
    row = lax.broadcasted_iota(jnp.int32, (SPARE, one.shape[1]), 0)
    give[0, CHUNK:, :] = jnp.where(row == 0, one, jnp.where(row == 1, two, 0.0)).astype(low)


def early_terms(core, first_adj, layer_one, sums, bias_one, bias_two, lines):
    low, wide = jnp.bfloat16, jnp.float32
    rows, width = first_adj.shape
    rank = sums.shape[1]
    pairs = CHUNK // (2 * lines)
    chunks = width // CHUNK
    across = pl.BlockSpec((rows, CHUNK), lambda i, place: (0, i))
    line = pl.BlockSpec((1, CHUNK), lambda i, place: (0, i))
    return pl.pallas_call(
        early_kernel,
        grid_spec=pltpu.PrefetchScalarGridSpec(
            num_scalar_prefetch=1,
            grid=(chunks,),
            in_specs=[across, across, pl.BlockSpec(sums.shape, lambda i, place: (0, 0)), line, line],
            out_specs=[
                pl.BlockSpec((CHUNK, rank // 2), lambda i, place: (i, 0)),
                pl.BlockSpec((pairs, lines, rank), lambda i, place: (i, 0, 0)),
                pl.BlockSpec((1, CHUNK + SPARE, rank), lambda i, place: (i, 0, 0)),
            ],
        ),
        out_shape=[
            pltpu.HBM((width, rank // 2), wide),
            pltpu.HBM((width // (2 * lines), lines, rank), wide),
            pltpu.HBM((chunks, CHUNK + SPARE, rank), low),
        ],
        compiler_params=PARAMS,
    )(core[None], in_hbm(first_adj), in_hbm(layer_one), sums, bias_one, bias_two)


def finish_kernel(keep_u, give_u, keep_v, peer, bias_one, bias_two, sent):
    low, wide = sent.dtype, jnp.float32
    chips, lines, rank = keep_v.shape
    half_rank = rank // 2
    chunks = peer.shape[0]
    pairs = chips // chunks
    tail = jnp.zeros((SPARE, rank), wide)
    row = lax.broadcasted_iota(jnp.int32, tail.shape, 0)
    for i in range(chunks):
        for pair in range(pairs):
            top = 2 * pair * lines
            left = peer[i, top : top + lines, half_rank:].astype(wide)
            right = peer[i, top + lines : top + 2 * lines, half_rank:].astype(wide)
            chip = i * pairs + pair
            sent[chip, :lines, :] = (keep_u[chip] + give_u[chip].astype(wide)).astype(low)
            sent[chip, lines : 2 * lines, :half_rank] = (keep_v[chip, :, :half_rank] + left).astype(low)
            sent[chip, lines : 2 * lines, half_rank:] = (keep_v[chip, :, half_rank:] + right).astype(low)
        theirs = peer[i, CHUNK:, :].astype(wide)
        theirs = theirs[:, :half_rank] + theirs[:, half_rank:]
        spot = slice(i * CHUNK, (i + 1) * CHUNK)
        for t, bias in enumerate((bias_one, bias_two)):
            high, rest = in_two(bias[:, spot])
            line = jnp.concatenate(in_two((high + rest) + theirs[t : t + 1]), 1)
            tail = jnp.where(row == 2 * i + t, line, tail)
    for chip in range(chips):
        sent[chip, 2 * lines :, :] = tail.astype(low)


def finished(keep_u, peer_u, keep_v, peer, bias_one, bias_two):
    chips, lines, rank = keep_v.shape
    return pl.pallas_call(
        finish_kernel,
        out_shape=jax.ShapeDtypeStruct((chips, 2 * lines + SPARE, rank), jnp.bfloat16),
        compiler_params=PARAMS,
    )(keep_u, peer_u, keep_v, peer, bias_one, bias_two)


def late_kernel(place, second_adj, sums, keep, give):
    rows = second_adj.shape[0]
    pairs, lines, _ = keep.shape
    term = transposed_dot(second_adj[...], sums[:rows, :])
    for pair in range(pairs):
        keep[pair], away = halves_of(term, place[0], pair, lines)
        give[pair] = away.astype(give.dtype)


def late_terms(core, second_adj, sums, lines):
    rows, width = second_adj.shape
    rank = sums.shape[1]
    shared = pl.BlockSpec((CHUNK // (2 * lines), lines, rank), lambda i, place: (i, 0, 0))
    shape = (width // (2 * lines), lines, rank)
    return pl.pallas_call(
        late_kernel,
        grid_spec=pltpu.PrefetchScalarGridSpec(
            num_scalar_prefetch=1,
            grid=(width // CHUNK,),
            in_specs=[
                pl.BlockSpec((rows, CHUNK), lambda i, place: (0, i)),
                pl.BlockSpec(sums.shape, lambda i, place: (0, 0)),
            ],
            out_specs=[shared, shared],
        ),
        out_shape=[jax.ShapeDtypeStruct(shape, jnp.float32), jax.ShapeDtypeStruct(shape, jnp.bfloat16)],
        compiler_params=PARAMS,
    )(core[None], second_adj, sums)


def last_kernel(lines, taken, grad_su, grad_sv, grad_bias):
    low, wide = jnp.bfloat16, jnp.float32
    total = jnp.sum(taken[...].astype(wide), axis=0)
    grad_su[...] = total[:lines].astype(low)
    grad_sv[...] = total[lines : 2 * lines].astype(low)
    sums = total[2 * lines :]
    sums = sums[:, : sums.shape[1] // 2] + sums[:, sums.shape[1] // 2 :]
    for i in range(grad_bias.shape[1] // CHUNK):
        grad_bias[:, i * CHUNK : (i + 1) * CHUNK] = sums[2 * i : 2 * i + 2]


def last_sum(taken, lines, width):
    rank = taken.shape[2]
    return pl.pallas_call(
        functools.partial(last_kernel, lines),
        out_shape=[
            jax.ShapeDtypeStruct((lines, rank), jnp.bfloat16),
            jax.ShapeDtypeStruct((lines, rank), jnp.bfloat16),
            jax.ShapeDtypeStruct((2, width), jnp.float32),
        ],
        compiler_params=PARAMS,
    )(taken)


def local(x0, cotangent, domain_ids, expert_u, expert_v, shared_u, shared_v, bias):
    low = jnp.bfloat16
    wide = jnp.float32
    rows, width = x0.shape
    half_rank = expert_u.shape[1]
    rank = 2 * half_rank
    chips = lax.axis_size("dom") // 2
    lines = shared_u.shape[0]
    domain = lax.axis_index("dom") // 2
    core = lax.axis_index("dom") % 2

    maps = spread(shared_u, shared_v, chips)
    maps, expert_u, expert_v = lax.optimization_barrier((maps, expert_u, expert_v))
    own_maps = exchange(maps.reshape(-1, rank), "dom", chip_groups()).reshape(maps.shape)
    other_v = core_swap(expert_v)
    other_u = core_swap(expert_u)
    full_v = jnp.concatenate([expert_v, other_v], 1)

    masked = jnp.where((domain_ids == domain)[:, None], cotangent, jnp.zeros_like(cotangent))
    second_adj = (masked.astype(wide) * x0.astype(wide)).astype(low)
    bias_two = jnp.sum(second_adj.astype(wide), axis=0, keepdims=True)

    first_part = dot(x0, full_v).astype(low)
    own_maps, first_part, second_adj, bias_two = lax.optimization_barrier((own_maps, first_part, second_adj, bias_two))
    other_maps = core_swap(own_maps)
    own_su, other_su = own_maps[:, :lines], other_maps[:, :lines]
    pair = [jnp.where(core == 0, own_su, other_su), jnp.where(core == 0, other_su, own_su)]
    whole_su = jnp.stack(pair, 1).reshape(width, rank)
    back_two_part = dot(second_adj, whole_su).astype(low)
    both = jnp.concatenate([first_part, back_two_part], 0)
    near, ring = near_groups(), ring_groups()
    other_u, both = lax.optimization_barrier((other_u, both))
    part = summed(summed(both, "feat", near), "feat", ring)
    sums = gathered(gathered(part, "feat", ring), "feat", near)

    both, layer_one, first_adj, kept, bias_one = middle(
        core, sums, x0, masked, expert_u, other_u, own_maps, other_maps, bias
    )
    keep_eu, keep_sv, give = early_terms(core, first_adj, layer_one, sums, bias_one, bias_two, lines)
    part = summed(both, "feat", near)
    part, give = lax.optimization_barrier((part, give))
    part = summed(part, "feat", ring)
    part, give = lax.optimization_barrier((gathered(part, "feat", ring), give))
    peer = core_swap(give)
    sums = gathered(part, "feat", near)

    keep_su, give_su = late_terms(core, second_adj, sums, lines)
    sent = finished(keep_su, core_swap(give_su), keep_sv, peer, bias_one, bias_two)
    sent, sums = lax.optimization_barrier((sent, sums))
    taken = exchange(sent.reshape(-1, rank), "dom", chip_groups()).reshape(sent.shape)
    peer_eu = peer[:, :CHUNK, :half_rank].reshape(width, half_rank)
    grad_eu = (keep_eu + peer_eu.astype(wide)).astype(low)
    second_rank, back_one = sums[:rows], sums[rows:]
    partial_ev = transposed_dot(x0, back_one)
    peer_ev = core_swap(partial_ev[:, half_rank:].astype(low))
    grad_ev = (partial_ev[:, :half_rank] + peer_ev.astype(wide)).astype(low)
    second_gate = cross_dot(second_rank, whole_su) + bias[1][None, :]
    grad_inputs = (masked.astype(wide) * second_gate + kept + cross_dot(back_one, full_v)).astype(low)
    grad_su, grad_sv, grad_bias = last_sum(taken, lines, width)
    return (grad_inputs, grad_eu, grad_ev, grad_su, grad_sv, grad_bias)


def solution(mesh):
    placed = (
        P("dom", "feat"),
        P("dom", "feat"),
        P("dom"),
        P("feat", "dom"),
        P("feat", "dom"),
        P(("feat", "dom"), None),
        P(("feat", "dom"), None),
        P(None, "feat"),
    )
    return jax.shard_map(
        local,
        mesh=mesh,
        in_specs=placed,
        out_specs=(
            P("dom", "feat"),
            P("feat", "dom"),
            P("feat", "dom"),
            P(("feat", "dom"), None),
            P(("feat", "dom"), None),
            P(None, "feat"),
        ),
        check_vma=False,
    )
```

```python
import functools

import jax
import jax.numpy as jnp
from jax import lax
from jax.experimental import pallas as pl
from jax.experimental.pallas import tpu as pltpu
from jax.sharding import PartitionSpec as P

FAR = 2
CHUNK = 256
MIDDLE_CHUNK = 512
SPARE = 16
PARAMS = pltpu.CompilerParams(vmem_limit_bytes=32 * 1024 * 1024)


def core_swap(value):
    pairs = [(source, source ^ 1) for source in range(lax.axis_size("dom"))]
    return lax.ppermute(value, "dom", pairs)


def near_groups():
    half = lax.axis_size("feat") // FAR
    return [[far * half + 2 * pair + bit for far in range(FAR) for bit in range(2)] for pair in range(half // 2)]


def ring_groups():
    half = lax.axis_size("feat") // FAR
    return [[far * half + 2 * step + bit for step in range(half // 2)] for far in range(FAR) for bit in range(2)]


def chip_groups():
    return [list(range(core, lax.axis_size("dom"), 2)) for core in range(2)]


def exchange(value, axis, groups):
    return lax.all_to_all(value, axis, 0, 0, axis_index_groups=groups, tiled=True)


def gathered(value, axis, groups):
    members = len(groups[0])
    repeated = jnp.broadcast_to(value[None], (members, *value.shape))
    return exchange(repeated.reshape(members * value.shape[0], value.shape[1]), axis, groups)


def summed(value, axis, groups):
    pieces = exchange(value, axis, groups).reshape(len(groups[0]), -1, value.shape[1])
    return jnp.sum(pieces.astype(jnp.float32), axis=0).astype(jnp.bfloat16)


def dot(left_side, right_side):
    return jnp.dot(left_side, right_side, preferred_element_type=jnp.float32)


def transposed_dot(left_side, right_side):
    return lax.dot_general(
        left_side, right_side, (((0,), (0,)), ((), ())), preferred_element_type=jnp.float32
    )


def cross_dot(left_side, right_side):
    return lax.dot_general(
        left_side, right_side, (((1,), (1,)), ((), ())), preferred_element_type=jnp.float32
    )


def in_hbm(value):
    return pltpu.with_memory_space_constraint(value, pltpu.HBM)


def middle_kernel(
    place, sums, x0, masked, own_u, other_u, own_v, other_v, bias, both, layer_one, first_adj, kept, bias_sum, total, map_v
):
    low, wide = jnp.bfloat16, jnp.float32
    rows, half_rank = x0.shape[0], own_u.shape[1]
    chips, lines, _ = own_v.shape
    step = pl.program_id(0)

    def fill(pair):
        for chip in range(chips):
            for i, part in enumerate(pair):
                top = (2 * chip + i) * lines
                map_v[top : top + lines, :] = part[chip]

    @pl.when(place[0] == 0)
    def _():
        fill((own_v, other_v))

    @pl.when(place[0] != 0)
    def _():
        fill((other_v, own_v))

    inputs = x0[...].astype(wide)
    first_gate = (
        cross_dot(sums[:rows, :half_rank], own_u[...])
        + cross_dot(sums[:rows, half_rank:], other_u[...])
        + bias[:1, :]
    )
    layer = (inputs * first_gate + inputs).astype(low)
    layer_grad = masked[...].astype(wide) + cross_dot(sums[rows:, :], map_v[...])
    adj = (layer_grad * inputs).astype(low)
    layer_one[...] = layer
    first_adj[...] = adj
    kept[...] = layer_grad * (first_gate + 1.0)
    bias_sum[...] = jnp.sum(adj.astype(wide), axis=0, keepdims=True)
    parts = (
        (slice(0, rows), slice(None), dot(layer, map_v[...])),
        (slice(rows, None), slice(0, half_rank), dot(adj, own_u[...])),
        (slice(rows, None), slice(half_rank, None), dot(adj, other_u[...])),
    )
    last = pl.num_programs(0) - 1

    @pl.when(step == 0)
    def _():
        for across, along, part in parts:
            total[across, along] = part

    @pl.when(jnp.logical_and(step > 0, step < last))
    def _():
        for across, along, part in parts:
            total[across, along] += part

    @pl.when(step == last)
    def _():
        for across, along, part in parts:
            both[across, along] = (total[across, along] + part).astype(low)


def middle(core, sums, x0, masked, own_u, other_u, own_maps, other_maps, bias):
    low, wide = jnp.bfloat16, jnp.float32
    rows, width = x0.shape
    rank = sums.shape[1]
    lines = own_maps.shape[1] // 2
    across = pl.BlockSpec((rows, MIDDLE_CHUNK), lambda i, place: (0, i))
    half = pl.BlockSpec((MIDDLE_CHUNK, rank // 2), lambda i, place: (i, 0))
    fixed = pl.BlockSpec((2 * rows, rank), lambda i, place: (0, 0))
    map_rows = pl.BlockSpec((MIDDLE_CHUNK // (2 * lines), lines, rank), lambda i, place: (i, 1, 0))
    return pl.pallas_call(
        middle_kernel,
        grid_spec=pltpu.PrefetchScalarGridSpec(
            num_scalar_prefetch=1,
            grid=(width // MIDDLE_CHUNK,),
            in_specs=[
                fixed,
                across,
                across,
                half,
                half,
                map_rows,
                map_rows,
                pl.BlockSpec((2, MIDDLE_CHUNK), lambda i, place: (0, i)),
            ],
            out_specs=[fixed, across, across, across, pl.BlockSpec((1, MIDDLE_CHUNK), lambda i, place: (0, i))],
            scratch_shapes=[pltpu.VMEM((2 * rows, rank), wide), pltpu.VMEM((MIDDLE_CHUNK, rank), low)],
        ),
        out_shape=[
            pltpu.HBM((2 * rows, rank), low),
            pltpu.HBM((rows, width), low),
            pltpu.HBM((rows, width), low),
            pltpu.HBM((rows, width), wide),
            jax.ShapeDtypeStruct((1, width), wide),
        ],
        compiler_params=PARAMS,
    )(core[None], sums, x0, masked, own_u, other_u, own_maps, other_maps, bias)


def spread_kernel(map_u, map_v, out):
    lines = map_u.shape[0]
    for chip in range(out.shape[0]):
        out[chip, :lines, :] = map_u[...]
        out[chip, lines:, :] = map_v[...]


def spread(map_u, map_v, chips):
    lines, rank = map_u.shape
    rows = pl.BlockSpec((lines, rank), lambda i: (0, 0))
    return pl.pallas_call(
        spread_kernel,
        grid=(2,),
        in_specs=[rows, rows],
        out_specs=pl.BlockSpec((chips // 2, 2 * lines, rank), lambda i: (i, 0, 0)),
        out_shape=jax.ShapeDtypeStruct((chips, 2 * lines, rank), map_u.dtype),
        compiler_params=PARAMS,
    )(in_hbm(map_u), in_hbm(map_v))


def halves_of(term, core, pair, lines):
    first = term[2 * pair * lines : (2 * pair + 1) * lines]
    second = term[(2 * pair + 1) * lines : (2 * pair + 2) * lines]
    return jnp.where(core == 0, first, second), jnp.where(core == 0, second, first)


def in_two(line):
    high = line.astype(jnp.bfloat16).astype(jnp.float32)
    return high, (line - high).astype(jnp.bfloat16).astype(jnp.float32)


def early_kernel(place, first_adj, layer_one, sums, bias_one, bias_two, keep_u, keep_v, give):
    low = give.dtype
    rows, half_rank = first_adj.shape[0], keep_u.shape[1]
    pairs, lines, _ = keep_v.shape
    keep_u[...] = transposed_dot(first_adj[...], sums[:rows, :half_rank])
    give[0, :CHUNK, :half_rank] = transposed_dot(first_adj[...], sums[:rows, half_rank:]).astype(low)
    term = transposed_dot(layer_one[...], sums[rows:, :])
    for pair in range(pairs):
        keep_v[pair], away = halves_of(term, place[0], pair, lines)
        top = 2 * pair * lines
        give[0, top : top + lines, half_rank:] = away[:, :half_rank].astype(low)
        give[0, top + lines : top + 2 * lines, half_rank:] = away[:, half_rank:].astype(low)
    one = jnp.concatenate(in_two(bias_one[...]), 1)
    two = jnp.concatenate(in_two(bias_two[...]), 1)
    row = lax.broadcasted_iota(jnp.int32, (SPARE, one.shape[1]), 0)
    give[0, CHUNK:, :] = jnp.where(row == 0, one, jnp.where(row == 1, two, 0.0)).astype(low)


def early_terms(core, first_adj, layer_one, sums, bias_one, bias_two, lines):
    low, wide = jnp.bfloat16, jnp.float32
    rows, width = first_adj.shape
    rank = sums.shape[1]
    pairs = CHUNK // (2 * lines)
    chunks = width // CHUNK
    across = pl.BlockSpec((rows, CHUNK), lambda i, place: (0, i))
    line = pl.BlockSpec((1, CHUNK), lambda i, place: (0, i))
    return pl.pallas_call(
        early_kernel,
        grid_spec=pltpu.PrefetchScalarGridSpec(
            num_scalar_prefetch=1,
            grid=(chunks,),
            in_specs=[across, across, pl.BlockSpec(sums.shape, lambda i, place: (0, 0)), line, line],
            out_specs=[
                pl.BlockSpec((CHUNK, rank // 2), lambda i, place: (i, 0)),
                pl.BlockSpec((pairs, lines, rank), lambda i, place: (i, 0, 0)),
                pl.BlockSpec((1, CHUNK + SPARE, rank), lambda i, place: (i, 0, 0)),
            ],
        ),
        out_shape=[
            pltpu.HBM((width, rank // 2), wide),
            pltpu.HBM((width // (2 * lines), lines, rank), wide),
            pltpu.HBM((chunks, CHUNK + SPARE, rank), low),
        ],
        compiler_params=PARAMS,
    )(core[None], in_hbm(first_adj), in_hbm(layer_one), sums, bias_one, bias_two)


def finish_kernel(keep_u, give_u, keep_v, peer, bias_one, bias_two, sent):
    low, wide = sent.dtype, jnp.float32
    chips, lines, rank = keep_v.shape
    half_rank = rank // 2
    chunks = peer.shape[0]
    pairs = chips // chunks
    tail = jnp.zeros((SPARE, rank), wide)
    row = lax.broadcasted_iota(jnp.int32, tail.shape, 0)
    for i in range(chunks):
        for pair in range(pairs):
            top = 2 * pair * lines
            left = peer[i, top : top + lines, half_rank:].astype(wide)
            right = peer[i, top + lines : top + 2 * lines, half_rank:].astype(wide)
            chip = i * pairs + pair
            sent[chip, :lines, :] = (keep_u[chip] + give_u[chip].astype(wide)).astype(low)
            sent[chip, lines : 2 * lines, :half_rank] = (keep_v[chip, :, :half_rank] + left).astype(low)
            sent[chip, lines : 2 * lines, half_rank:] = (keep_v[chip, :, half_rank:] + right).astype(low)
        theirs = peer[i, CHUNK:, :].astype(wide)
        theirs = theirs[:, :half_rank] + theirs[:, half_rank:]
        spot = slice(i * CHUNK, (i + 1) * CHUNK)
        for t, bias in enumerate((bias_one, bias_two)):
            high, rest = in_two(bias[:, spot])
            line = jnp.concatenate(in_two((high + rest) + theirs[t : t + 1]), 1)
            tail = jnp.where(row == 2 * i + t, line, tail)
    for chip in range(chips):
        sent[chip, 2 * lines :, :] = tail.astype(low)


def finished(keep_u, peer_u, keep_v, peer, bias_one, bias_two):
    chips, lines, rank = keep_v.shape
    return pl.pallas_call(
        finish_kernel,
        out_shape=jax.ShapeDtypeStruct((chips, 2 * lines + SPARE, rank), jnp.bfloat16),
        compiler_params=PARAMS,
    )(keep_u, peer_u, keep_v, peer, bias_one, bias_two)


def late_kernel(place, second_adj, sums, keep, give):
    rows = second_adj.shape[0]
    pairs, lines, _ = keep.shape
    term = transposed_dot(second_adj[...], sums[:rows, :])
    for pair in range(pairs):
        keep[pair], away = halves_of(term, place[0], pair, lines)
        give[pair] = away.astype(give.dtype)


def late_terms(core, second_adj, sums, lines):
    rows, width = second_adj.shape
    rank = sums.shape[1]
    shared = pl.BlockSpec((CHUNK // (2 * lines), lines, rank), lambda i, place: (i, 0, 0))
    shape = (width // (2 * lines), lines, rank)
    return pl.pallas_call(
        late_kernel,
        grid_spec=pltpu.PrefetchScalarGridSpec(
            num_scalar_prefetch=1,
            grid=(width // CHUNK,),
            in_specs=[
                pl.BlockSpec((rows, CHUNK), lambda i, place: (0, i)),
                pl.BlockSpec(sums.shape, lambda i, place: (0, 0)),
            ],
            out_specs=[shared, shared],
        ),
        out_shape=[jax.ShapeDtypeStruct(shape, jnp.float32), jax.ShapeDtypeStruct(shape, jnp.bfloat16)],
        compiler_params=PARAMS,
    )(core[None], second_adj, sums)


def last_kernel(lines, taken, grad_su, grad_sv, grad_bias):
    low, wide = jnp.bfloat16, jnp.float32
    total = jnp.sum(taken[...].astype(wide), axis=0)
    grad_su[...] = total[:lines].astype(low)
    grad_sv[...] = total[lines : 2 * lines].astype(low)
    sums = total[2 * lines :]
    sums = sums[:, : sums.shape[1] // 2] + sums[:, sums.shape[1] // 2 :]
    for i in range(grad_bias.shape[1] // CHUNK):
        grad_bias[:, i * CHUNK : (i + 1) * CHUNK] = sums[2 * i : 2 * i + 2]


def last_sum(taken, lines, width):
    rank = taken.shape[2]
    return pl.pallas_call(
        functools.partial(last_kernel, lines),
        out_shape=[
            jax.ShapeDtypeStruct((lines, rank), jnp.bfloat16),
            jax.ShapeDtypeStruct((lines, rank), jnp.bfloat16),
            jax.ShapeDtypeStruct((2, width), jnp.float32),
        ],
        compiler_params=PARAMS,
    )(taken)


def local(x0, cotangent, domain_ids, expert_u, expert_v, shared_u, shared_v, bias):
    low = jnp.bfloat16
    wide = jnp.float32
    rows, width = x0.shape
    half_rank = expert_u.shape[1]
    rank = 2 * half_rank
    chips = lax.axis_size("dom") // 2
    lines = shared_u.shape[0]
    domain = lax.axis_index("dom") // 2
    core = lax.axis_index("dom") % 2

    maps = spread(shared_u, shared_v, chips)
    maps, expert_u, expert_v = lax.optimization_barrier((maps, expert_u, expert_v))
    own_maps = exchange(maps.reshape(-1, rank), "dom", chip_groups()).reshape(maps.shape)
    other_v = core_swap(expert_v)
    other_u = core_swap(expert_u)
    full_v = jnp.concatenate([expert_v, other_v], 1)

    masked = jnp.where((domain_ids == domain)[:, None], cotangent, jnp.zeros_like(cotangent))
    second_adj = (masked.astype(wide) * x0.astype(wide)).astype(low)
    bias_two = jnp.sum(second_adj.astype(wide), axis=0, keepdims=True)

    first_part = dot(x0, full_v).astype(low)
    own_maps, first_part, second_adj, bias_two = lax.optimization_barrier((own_maps, first_part, second_adj, bias_two))
    other_maps = core_swap(own_maps)
    own_su, other_su = own_maps[:, :lines], other_maps[:, :lines]
    pair = [jnp.where(core == 0, own_su, other_su), jnp.where(core == 0, other_su, own_su)]
    whole_su = jnp.stack(pair, 1).reshape(width, rank)
    back_two_part = dot(second_adj, whole_su).astype(low)
    both = jnp.concatenate([first_part, back_two_part], 0)
    near, ring = near_groups(), ring_groups()
    other_u, both = lax.optimization_barrier((other_u, both))
    part = summed(summed(both, "feat", near), "feat", ring)
    sums = gathered(gathered(part, "feat", ring), "feat", near)

    both, layer_one, first_adj, kept, bias_one = middle(
        core, sums, x0, masked, expert_u, other_u, own_maps, other_maps, bias
    )
    keep_eu, keep_sv, give = early_terms(core, first_adj, layer_one, sums, bias_one, bias_two, lines)
    part = summed(both, "feat", near)
    part, give = lax.optimization_barrier((part, give))
    part = summed(part, "feat", ring)
    part, give = lax.optimization_barrier((gathered(part, "feat", ring), give))
    peer = core_swap(give)
    sums = gathered(part, "feat", near)

    keep_su, give_su = late_terms(core, second_adj, sums, lines)
    sent = finished(keep_su, core_swap(give_su), keep_sv, peer, bias_one, bias_two)
    sent, sums = lax.optimization_barrier((sent, sums))
    taken = exchange(sent.reshape(-1, rank), "dom", chip_groups()).reshape(sent.shape)
    peer_eu = peer[:, :CHUNK, :half_rank].reshape(width, half_rank)
    grad_eu = (keep_eu + peer_eu.astype(wide)).astype(low)
    second_rank, back_one = sums[:rows], sums[rows:]
    partial_ev = transposed_dot(x0, back_one)
    peer_ev = core_swap(partial_ev[:, half_rank:].astype(low))
    grad_ev = (partial_ev[:, :half_rank] + peer_ev.astype(wide)).astype(low)
    second_gate = cross_dot(second_rank, whole_su) + bias[1][None, :]
    grad_inputs = (masked.astype(wide) * second_gate + kept + cross_dot(back_one, full_v)).astype(low)
    grad_su, grad_sv, grad_bias = last_sum(taken, lines, width)
    return (grad_inputs, grad_eu, grad_ev, grad_su, grad_sv, grad_bias)


def solution(mesh):
    placed = (
        P("dom", "feat"),
        P("dom", "feat"),
        P("dom"),
        P("feat", "dom"),
        P("feat", "dom"),
        P(("feat", "dom"), None),
        P(("feat", "dom"), None),
        P(None, "feat"),
    )
    return jax.shard_map(
        local,
        mesh=mesh,
        in_specs=placed,
        out_specs=(
            P("dom", "feat"),
            P("feat", "dom"),
            P("feat", "dom"),
            P(("feat", "dom"), None),
            P(("feat", "dom"), None),
            P(None, "feat"),
        ),
        check_vma=False,
    )
```

```python
import functools

import jax
import jax.numpy as jnp
from jax import lax
from jax.experimental import pallas as pl
from jax.experimental.pallas import tpu as pltpu
from jax.sharding import PartitionSpec as P

FAR = 2
CHUNK = 256
MIDDLE_CHUNK = 512
SPARE = 16
PARAMS = pltpu.CompilerParams(vmem_limit_bytes=32 * 1024 * 1024)


def core_swap(value):
    pairs = [(source, source ^ 1) for source in range(lax.axis_size("dom"))]
    return lax.ppermute(value, "dom", pairs)


def near_groups():
    half = lax.axis_size("feat") // FAR
    return [[far * half + 2 * pair + bit for far in range(FAR) for bit in range(2)] for pair in range(half // 2)]


def ring_groups():
    half = lax.axis_size("feat") // FAR
    return [[far * half + 2 * step + bit for step in range(half // 2)] for far in range(FAR) for bit in range(2)]


def chip_groups():
    return [list(range(core, lax.axis_size("dom"), 2)) for core in range(2)]


def exchange(value, axis, groups):
    return lax.all_to_all(value, axis, 0, 0, axis_index_groups=groups, tiled=True)


def gathered(value, axis, groups):
    members = len(groups[0])
    repeated = jnp.broadcast_to(value[None], (members, *value.shape))
    return exchange(repeated.reshape(members * value.shape[0], value.shape[1]), axis, groups)


def summed(value, axis, groups):
    pieces = exchange(value, axis, groups).reshape(len(groups[0]), -1, value.shape[1])
    return jnp.sum(pieces.astype(jnp.float32), axis=0).astype(jnp.bfloat16)


def dot(left_side, right_side):
    return jnp.dot(left_side, right_side, preferred_element_type=jnp.float32)


def transposed_dot(left_side, right_side):
    return lax.dot_general(
        left_side, right_side, (((0,), (0,)), ((), ())), preferred_element_type=jnp.float32
    )


def cross_dot(left_side, right_side):
    return lax.dot_general(
        left_side, right_side, (((1,), (1,)), ((), ())), preferred_element_type=jnp.float32
    )


def in_hbm(value):
    return pltpu.with_memory_space_constraint(value, pltpu.HBM)


def middle_kernel(
    place, sums, x0, masked, own_u, other_u, own_v, other_v, bias, both, layer_one, first_adj, kept, bias_sum, total, map_v
):
    low, wide = jnp.bfloat16, jnp.float32
    rows, half_rank = x0.shape[0], own_u.shape[1]
    chips, lines, _ = own_v.shape
    step = pl.program_id(0)

    def fill(pair):
        for chip in range(chips):
            for i, part in enumerate(pair):
                top = (2 * chip + i) * lines
                map_v[top : top + lines, :] = part[chip]

    @pl.when(place[0] == 0)
    def _():
        fill((own_v, other_v))

    @pl.when(place[0] != 0)
    def _():
        fill((other_v, own_v))

    inputs = x0[...].astype(wide)
    first_gate = (
        cross_dot(sums[:rows, :half_rank], own_u[...])
        + cross_dot(sums[:rows, half_rank:], other_u[...])
        + bias[:1, :]
    )
    layer = (inputs * first_gate + inputs).astype(low)
    layer_grad = masked[...].astype(wide) + cross_dot(sums[rows:, :], map_v[...])
    adj = (layer_grad * inputs).astype(low)
    layer_one[...] = layer
    first_adj[...] = adj
    kept[...] = layer_grad * (first_gate + 1.0)
    bias_sum[...] = jnp.sum(adj.astype(wide), axis=0, keepdims=True)
    parts = (
        (slice(0, rows), slice(None), dot(layer, map_v[...])),
        (slice(rows, None), slice(0, half_rank), dot(adj, own_u[...])),
        (slice(rows, None), slice(half_rank, None), dot(adj, other_u[...])),
    )
    last = pl.num_programs(0) - 1

    @pl.when(step == 0)
    def _():
        for across, along, part in parts:
            total[across, along] = part

    @pl.when(jnp.logical_and(step > 0, step < last))
    def _():
        for across, along, part in parts:
            total[across, along] += part

    @pl.when(step == last)
    def _():
        for across, along, part in parts:
            both[across, along] = (total[across, along] + part).astype(low)


def middle(core, sums, x0, masked, own_u, other_u, own_maps, other_maps, bias):
    low, wide = jnp.bfloat16, jnp.float32
    rows, width = x0.shape
    rank = sums.shape[1]
    lines = own_maps.shape[1] // 2
    across = pl.BlockSpec((rows, MIDDLE_CHUNK), lambda i, place: (0, i))
    half = pl.BlockSpec((MIDDLE_CHUNK, rank // 2), lambda i, place: (i, 0))
    fixed = pl.BlockSpec((2 * rows, rank), lambda i, place: (0, 0))
    map_rows = pl.BlockSpec((MIDDLE_CHUNK // (2 * lines), lines, rank), lambda i, place: (i, 1, 0))
    return pl.pallas_call(
        middle_kernel,
        grid_spec=pltpu.PrefetchScalarGridSpec(
            num_scalar_prefetch=1,
            grid=(width // MIDDLE_CHUNK,),
            in_specs=[
                fixed,
                across,
                across,
                half,
                half,
                map_rows,
                map_rows,
                pl.BlockSpec((2, MIDDLE_CHUNK), lambda i, place: (0, i)),
            ],
            out_specs=[fixed, across, across, across, pl.BlockSpec((1, MIDDLE_CHUNK), lambda i, place: (0, i))],
            scratch_shapes=[pltpu.VMEM((2 * rows, rank), wide), pltpu.VMEM((MIDDLE_CHUNK, rank), low)],
        ),
        out_shape=[
            pltpu.HBM((2 * rows, rank), low),
            pltpu.HBM((rows, width), low),
            pltpu.HBM((rows, width), low),
            pltpu.HBM((rows, width), wide),
            jax.ShapeDtypeStruct((1, width), wide),
        ],
        compiler_params=PARAMS,
    )(core[None], sums, *map(in_hbm, (x0, masked, own_u, other_u, own_maps, other_maps)), bias)


def spread_kernel(map_u, map_v, out):
    lines = map_u.shape[0]
    for chip in range(out.shape[0]):
        out[chip, :lines, :] = map_u[...]
        out[chip, lines:, :] = map_v[...]


def spread(map_u, map_v, chips):
    lines, rank = map_u.shape
    rows = pl.BlockSpec((lines, rank), lambda i: (0, 0))
    return pl.pallas_call(
        spread_kernel,
        grid=(2,),
        in_specs=[rows, rows],
        out_specs=pl.BlockSpec((chips // 2, 2 * lines, rank), lambda i: (i, 0, 0)),
        out_shape=jax.ShapeDtypeStruct((chips, 2 * lines, rank), map_u.dtype),
        compiler_params=PARAMS,
    )(in_hbm(map_u), in_hbm(map_v))


def halves_of(term, core, pair, lines):
    first = term[2 * pair * lines : (2 * pair + 1) * lines]
    second = term[(2 * pair + 1) * lines : (2 * pair + 2) * lines]
    return jnp.where(core == 0, first, second), jnp.where(core == 0, second, first)


def in_two(line):
    high = line.astype(jnp.bfloat16).astype(jnp.float32)
    return high, (line - high).astype(jnp.bfloat16).astype(jnp.float32)


def early_kernel(place, first_adj, layer_one, sums, bias_one, bias_two, keep_u, keep_v, give):
    low = give.dtype
    rows, half_rank = first_adj.shape[0], keep_u.shape[1]
    pairs, lines, _ = keep_v.shape
    keep_u[...] = transposed_dot(first_adj[...], sums[:rows, :half_rank])
    give[0, :CHUNK, :half_rank] = transposed_dot(first_adj[...], sums[:rows, half_rank:]).astype(low)
    term = transposed_dot(layer_one[...], sums[rows:, :])
    for pair in range(pairs):
        keep_v[pair], away = halves_of(term, place[0], pair, lines)
        top = 2 * pair * lines
        give[0, top : top + lines, half_rank:] = away[:, :half_rank].astype(low)
        give[0, top + lines : top + 2 * lines, half_rank:] = away[:, half_rank:].astype(low)
    one = jnp.concatenate(in_two(bias_one[...]), 1)
    two = jnp.concatenate(in_two(bias_two[...]), 1)
    row = lax.broadcasted_iota(jnp.int32, (SPARE, one.shape[1]), 0)
    give[0, CHUNK:, :] = jnp.where(row == 0, one, jnp.where(row == 1, two, 0.0)).astype(low)


def early_terms(core, first_adj, layer_one, sums, bias_one, bias_two, lines):
    low, wide = jnp.bfloat16, jnp.float32
    rows, width = first_adj.shape
    rank = sums.shape[1]
    pairs = CHUNK // (2 * lines)
    chunks = width // CHUNK
    across = pl.BlockSpec((rows, CHUNK), lambda i, place: (0, i))
    line = pl.BlockSpec((1, CHUNK), lambda i, place: (0, i))
    return pl.pallas_call(
        early_kernel,
        grid_spec=pltpu.PrefetchScalarGridSpec(
            num_scalar_prefetch=1,
            grid=(chunks,),
            in_specs=[across, across, pl.BlockSpec(sums.shape, lambda i, place: (0, 0)), line, line],
            out_specs=[
                pl.BlockSpec((CHUNK, rank // 2), lambda i, place: (i, 0)),
                pl.BlockSpec((pairs, lines, rank), lambda i, place: (i, 0, 0)),
                pl.BlockSpec((1, CHUNK + SPARE, rank), lambda i, place: (i, 0, 0)),
            ],
        ),
        out_shape=[
            pltpu.HBM((width, rank // 2), wide),
            pltpu.HBM((width // (2 * lines), lines, rank), wide),
            pltpu.HBM((chunks, CHUNK + SPARE, rank), low),
        ],
        compiler_params=PARAMS,
    )(core[None], in_hbm(first_adj), in_hbm(layer_one), sums, bias_one, bias_two)


def finish_kernel(keep_u, give_u, keep_v, peer, bias_one, bias_two, sent):
    low, wide = sent.dtype, jnp.float32
    chips, lines, rank = keep_v.shape
    half_rank = rank // 2
    chunks = peer.shape[0]
    pairs = chips // chunks
    tail = jnp.zeros((SPARE, rank), wide)
    row = lax.broadcasted_iota(jnp.int32, tail.shape, 0)
    for i in range(chunks):
        for pair in range(pairs):
            top = 2 * pair * lines
            left = peer[i, top : top + lines, half_rank:].astype(wide)
            right = peer[i, top + lines : top + 2 * lines, half_rank:].astype(wide)
            chip = i * pairs + pair
            sent[chip, :lines, :] = (keep_u[chip] + give_u[chip].astype(wide)).astype(low)
            sent[chip, lines : 2 * lines, :half_rank] = (keep_v[chip, :, :half_rank] + left).astype(low)
            sent[chip, lines : 2 * lines, half_rank:] = (keep_v[chip, :, half_rank:] + right).astype(low)
        theirs = peer[i, CHUNK:, :].astype(wide)
        theirs = theirs[:, :half_rank] + theirs[:, half_rank:]
        spot = slice(i * CHUNK, (i + 1) * CHUNK)
        for t, bias in enumerate((bias_one, bias_two)):
            high, rest = in_two(bias[:, spot])
            line = jnp.concatenate(in_two((high + rest) + theirs[t : t + 1]), 1)
            tail = jnp.where(row == 2 * i + t, line, tail)
    for chip in range(chips):
        sent[chip, 2 * lines :, :] = tail.astype(low)


def finished(keep_u, peer_u, keep_v, peer, bias_one, bias_two):
    chips, lines, rank = keep_v.shape
    return pl.pallas_call(
        finish_kernel,
        out_shape=jax.ShapeDtypeStruct((chips, 2 * lines + SPARE, rank), jnp.bfloat16),
        compiler_params=PARAMS,
    )(keep_u, peer_u, keep_v, peer, bias_one, bias_two)


def late_kernel(place, second_adj, sums, keep, give):
    rows = second_adj.shape[0]
    pairs, lines, _ = keep.shape
    term = transposed_dot(second_adj[...], sums[:rows, :])
    for pair in range(pairs):
        keep[pair], away = halves_of(term, place[0], pair, lines)
        give[pair] = away.astype(give.dtype)


def late_terms(core, second_adj, sums, lines):
    rows, width = second_adj.shape
    rank = sums.shape[1]
    shared = pl.BlockSpec((CHUNK // (2 * lines), lines, rank), lambda i, place: (i, 0, 0))
    shape = (width // (2 * lines), lines, rank)
    return pl.pallas_call(
        late_kernel,
        grid_spec=pltpu.PrefetchScalarGridSpec(
            num_scalar_prefetch=1,
            grid=(width // CHUNK,),
            in_specs=[
                pl.BlockSpec((rows, CHUNK), lambda i, place: (0, i)),
                pl.BlockSpec(sums.shape, lambda i, place: (0, 0)),
            ],
            out_specs=[shared, shared],
        ),
        out_shape=[jax.ShapeDtypeStruct(shape, jnp.float32), jax.ShapeDtypeStruct(shape, jnp.bfloat16)],
        compiler_params=PARAMS,
    )(core[None], second_adj, sums)


def last_kernel(lines, taken, grad_su, grad_sv, grad_bias):
    low, wide = jnp.bfloat16, jnp.float32
    total = jnp.sum(taken[...].astype(wide), axis=0)
    grad_su[...] = total[:lines].astype(low)
    grad_sv[...] = total[lines : 2 * lines].astype(low)
    sums = total[2 * lines :]
    sums = sums[:, : sums.shape[1] // 2] + sums[:, sums.shape[1] // 2 :]
    for i in range(grad_bias.shape[1] // CHUNK):
        grad_bias[:, i * CHUNK : (i + 1) * CHUNK] = sums[2 * i : 2 * i + 2]


def last_sum(taken, lines, width):
    rank = taken.shape[2]
    return pl.pallas_call(
        functools.partial(last_kernel, lines),
        out_shape=[
            jax.ShapeDtypeStruct((lines, rank), jnp.bfloat16),
            jax.ShapeDtypeStruct((lines, rank), jnp.bfloat16),
            jax.ShapeDtypeStruct((2, width), jnp.float32),
        ],
        compiler_params=PARAMS,
    )(taken)


def local(x0, cotangent, domain_ids, expert_u, expert_v, shared_u, shared_v, bias):
    low = jnp.bfloat16
    wide = jnp.float32
    rows, width = x0.shape
    half_rank = expert_u.shape[1]
    rank = 2 * half_rank
    chips = lax.axis_size("dom") // 2
    lines = shared_u.shape[0]
    domain = lax.axis_index("dom") // 2
    core = lax.axis_index("dom") % 2

    maps = spread(shared_u, shared_v, chips)
    maps, expert_u, expert_v = lax.optimization_barrier((maps, expert_u, expert_v))
    own_maps = exchange(maps.reshape(-1, rank), "dom", chip_groups()).reshape(maps.shape)
    other_v = core_swap(expert_v)
    other_u = core_swap(expert_u)
    full_v = jnp.concatenate([expert_v, other_v], 1)

    masked = jnp.where((domain_ids == domain)[:, None], cotangent, jnp.zeros_like(cotangent))
    second_adj = (masked.astype(wide) * x0.astype(wide)).astype(low)
    bias_two = jnp.sum(second_adj.astype(wide), axis=0, keepdims=True)

    first_part = dot(x0, full_v).astype(low)
    own_maps, other_u, first_part, second_adj, bias_two = lax.optimization_barrier(
        (own_maps, other_u, first_part, second_adj, bias_two)
    )
    other_maps = core_swap(own_maps)
    own_su, other_su = own_maps[:, :lines], other_maps[:, :lines]
    pair = [jnp.where(core == 0, own_su, other_su), jnp.where(core == 0, other_su, own_su)]
    whole_su = jnp.stack(pair, 1).reshape(width, rank)
    back_two_part = dot(second_adj, whole_su).astype(low)
    both = jnp.concatenate([first_part, back_two_part], 0)
    near, ring = near_groups(), ring_groups()
    other_u, both = lax.optimization_barrier((other_u, both))
    part = summed(summed(both, "feat", near), "feat", ring)
    sums = gathered(gathered(part, "feat", ring), "feat", near)

    both, layer_one, first_adj, kept, bias_one = middle(
        core, sums, x0, masked, expert_u, other_u, own_maps, other_maps, bias
    )
    keep_eu, keep_sv, give = early_terms(core, first_adj, layer_one, sums, bias_one, bias_two, lines)
    part = summed(both, "feat", near)
    part, give = lax.optimization_barrier((part, give))
    part = summed(part, "feat", ring)
    part, give = lax.optimization_barrier((gathered(part, "feat", ring), give))
    peer = core_swap(give)
    sums = gathered(part, "feat", near)

    keep_su, give_su = late_terms(core, second_adj, sums, lines)
    sent = finished(keep_su, core_swap(give_su), keep_sv, peer, bias_one, bias_two)
    sent, sums = lax.optimization_barrier((sent, sums))
    taken = exchange(sent.reshape(-1, rank), "dom", chip_groups()).reshape(sent.shape)
    peer_eu = peer[:, :CHUNK, :half_rank].reshape(width, half_rank)
    grad_eu = (keep_eu + peer_eu.astype(wide)).astype(low)
    second_rank, back_one = sums[:rows], sums[rows:]
    partial_ev = transposed_dot(x0, back_one)
    peer_ev = core_swap(partial_ev[:, half_rank:].astype(low))
    grad_ev = (partial_ev[:, :half_rank] + peer_ev.astype(wide)).astype(low)
    second_gate = cross_dot(second_rank, whole_su) + bias[1][None, :]
    grad_inputs = (masked.astype(wide) * second_gate + kept + cross_dot(back_one, full_v)).astype(low)
    grad_su, grad_sv, grad_bias = last_sum(taken, lines, width)
    return (grad_inputs, grad_eu, grad_ev, grad_su, grad_sv, grad_bias)


def solution(mesh):
    placed = (
        P("dom", "feat"),
        P("dom", "feat"),
        P("dom"),
        P("feat", "dom"),
        P("feat", "dom"),
        P(("feat", "dom"), None),
        P(("feat", "dom"), None),
        P(None, "feat"),
    )
    return jax.shard_map(
        local,
        mesh=mesh,
        in_specs=placed,
        out_specs=(
            P("dom", "feat"),
            P("feat", "dom"),
            P("feat", "dom"),
            P(("feat", "dom"), None),
            P(("feat", "dom"), None),
            P(None, "feat"),
        ),
        check_vma=False,
    )
```
